256 devices in a mesh: cfg: 2 (over z_lo), ta: 4 (over y), ha: 4 (over x), wa: 8 (over z_hi, core).
Axes of the slice: x: 4, y: 4, z: 8 (z_hi: 4, z_lo: 2; z = z_hi * 2 + z_lo), core: 2. Of those that a mesh axis runs over, the one named last changes fastest.
Arguments:
- video_query: bfloat16 [2, 24, 32, 64, 1536], P('cfg', 'ta', 'ha', 'wa'), may hold values from -13.5 to 13.5
- video_key: bfloat16 [2, 24, 32, 64, 1536], P('cfg', 'ta', 'ha', 'wa'), may hold values from -13.5 to 13.5
- video_value: bfloat16 [2, 24, 32, 64, 1536], P('cfg', 'ta', 'ha', 'wa'), may hold values from -6 to 6
- text_query: bfloat16 [2, 128, 1536], P('cfg'), may hold values from -13.5 to 13.5
- text_key: bfloat16 [2, 128, 1536], P('cfg', ('ta', 'ha', 'wa')), may hold values from -9.5625 to 9.5625
- text_value: bfloat16 [2, 128, 1536], P('cfg', ('ta', 'ha', 'wa')), may hold values from -6 to 6
- text_count: int32 [2], P('cfg'), may hold values from 1 to 128, as said below
- head_windows: int32 [12, 3], replicated, may hold values from 1 to 3, as said below
- hidden_state: bfloat16 [2, 24, 32, 64, 3072], P('cfg', 'ta', 'ha', 'wa'), may hold values from -6 to 6
- out_weight: bfloat16 [1536, 3072], P('cfg'), may hold values from -0.15625 to 0.15625
- final_weight: bfloat16 [3072, 64], replicated, may hold values from -0.109375 to 0.109375
- modulation: float32 [2, 3, 3072], P('cfg'), may hold values from -4 to 4
- guidance: float32 [1], replicated, may hold values from 1.5 to 3
Outputs:
- patches: float32 [24, 32, 4096], P('ta', ('ha', 'cfg'), 'wa')
- text_attended: bfloat16 [2, 128, 1536], P('cfg')
The draws below stay inside these ranges and needn't reach their ends.
Inputs may be any that keep to these rules, and one draw needn't show every extreme that they name: `text_count`: branch 0 uses all 128 text positions; branch 1 uses at most 32. `head_windows`: every entry is 1 or 3; the columns are time, rows and columns. Exactly 3 heads have a 3 in some column, the others 1 in all three; some head has 3 in all three.
All inputs are finite; a program needn't handle non-finite values.
Results may differ from the reference program's by a relative error of at most 0.0034.
Values may be sent and summed in bfloat16 or wider, within the bound.
No kernel may reach another device: no remote copies, remote signals or barrier semaphores. Data moves between devices by JAX's collectives and lax.ppermute only.
A program may use at most 320 MiB of HBM per device.

```python
import math
import jax
import jax.numpy as jnp
from jax import lax

D = 3072
HEADS = 12
HEAD_DIM = 128
OUT_CH = 64
TILE_T = 6
TILE_H = 8
TILE_W = 8
L_TXT = 128
F = 1536
NT = 24
NH = 32
NW = 64


def draw_video_query(key, part):
    key = jax.random.fold_in(key, 1)
    base = jnp.clip(1.6 * jax.random.normal(key, (2, NT, NH, NW, F), jnp.float32), -9.6, 9.6)
    return base.astype(jnp.bfloat16)


def draw_video_key(key, part):
    key = jax.random.fold_in(key, 2)
    base = jnp.clip(1.6 * jax.random.normal(key, (2, NT, NH, NW, F), jnp.float32), -9.6, 9.6)
    return base.astype(jnp.bfloat16)


def draw_text_query(key, part):
    key = jax.random.fold_in(key, 3)
    base = jnp.clip(2.2 * jax.random.normal(key, (2, L_TXT, F), jnp.float32), -13.2, 13.2)
    return base.astype(jnp.bfloat16)


def draw_text_count(key, part):
    key = jax.random.fold_in(key, 4)
    short = jax.random.randint(key, (1,), 1, L_TXT // 4 + 1)
    return jnp.concatenate((jnp.full((1,), L_TXT, jnp.int32), short.astype(jnp.int32)))


def draw_head_windows(key, part):
    key = jax.random.fold_in(key, 5)
    first_key, second_key = jax.random.split(key)
    order = jax.random.permutation(first_key, HEADS)
    wide = order < HEADS // 4
    pattern = jax.random.randint(second_key, (HEADS,), 1, 8)
    pattern = jnp.where(order == 0, 7, pattern)
    pattern = jnp.where(wide, pattern, 0)
    bits = pattern[:, None] // jnp.array([1, 2, 4], jnp.int32)[None, :] % 2
    return (1 + 2 * bits).astype(jnp.int32)


def block_levels(own_key, shape, cuts, least, top_value):
    factor_of, own = 1.0, jax.random.fold_in(own_key, 6)
    for dim, shards_of in cuts:
        heights = jnp.exp(jax.random.uniform(jax.random.fold_in(own, dim), (shards_of,), jnp.float32, least / len(cuts), top_value / len(cuts)))
        factor_of = factor_of * jnp.repeat(heights, shape[dim] // shards_of).reshape([-1 if axis == dim else 1 for axis in range(len(shape))])
    return factor_of


def normal_values(rng, shape, spread, bound, cuts=(), kind=jnp.bfloat16):
    drawn = jax.random.normal(rng, shape, jnp.float32) * spread
    if len(cuts) > 0:
        drawn = block_levels(rng, shape, cuts, -0.22, 0.18) * drawn
    return jnp.clip(drawn, min=-bound, max=bound).astype(kind)


def setup_inputs(seed: int = 0) -> dict:
    key_list = jax.random.split(jax.random.key(seed), 14)
    return {
        "video_query": draw_video_query(jax.random.fold_in(key_list[13], 71), 0),
        "video_key": draw_video_key(jax.random.fold_in(key_list[13], 71), 0),
        "video_value": normal_values(key_list[2], (2, NT, NH, NW, F), 1.0, 6.0, ((0, 2), (1, 4), (2, 4), (3, 8))),
        "text_query": draw_text_query(jax.random.fold_in(key_list[13], 71), 0),
        "text_key": normal_values(key_list[4], (2, L_TXT, F), 1.6, 9.5625, ((0, 2), (1, 128))),
        "text_value": normal_values(key_list[5], (2, L_TXT, F), 1.0, 6.0, ((0, 2), (1, 128))),
        "text_count": draw_text_count(jax.random.fold_in(key_list[13], 71), 0),
        "head_windows": draw_head_windows(jax.random.fold_in(key_list[13], 71), 0),
        "hidden_state": normal_values(key_list[8], (2, NT, NH, NW, D), 1.0, 6.0, ((0, 2), (1, 4), (2, 4), (3, 8))),
        "out_weight": normal_values(key_list[9], (F, D), F ** -0.5, 0.15625, ((0, 2),)),
        "final_weight": normal_values(key_list[10], (D, OUT_CH), D ** -0.5, 0.109375),
        "modulation": normal_values(key_list[11], (2, 3, D), 1.0, 4.0, ((0, 2),), jnp.float32),
        "guidance": jnp.clip(jax.random.uniform(key_list[12], (1,), jnp.float32, 1.5, 3.0), 1.5, 3.0),
    }


def combine_parts(first, second):
    top = jnp.maximum(first[0], second[0])
    low = jnp.exp(first[0] - top)
    high = jnp.exp(second[0] - top)
    return (top, first[1] * low + second[1] * high, first[2] * low[..., None] + second[2] * high[..., None])

def masked_partial(scores, valid, values):
    held = jnp.where(valid, scores, -jnp.inf)
    peak = lax.optimization_barrier(jnp.max(held, axis=-1))
    weights = jnp.where(valid, jnp.exp(held - peak[..., None]), 0.0)
    total = lax.optimization_barrier(jnp.sum(weights, axis=-1))
    rounded = weights.astype(jnp.bfloat16).astype(jnp.float32)
    acc = jnp.einsum('hlk,khd->hld', rounded, values.astype(jnp.float32))
    return (peak, total, acc)

def reference(video_query, video_key, video_value, text_query, text_key, text_value, text_count, head_windows, hidden_state, out_weight, final_weight, modulation, guidance):
    inverse = 1.0 / math.sqrt(HEAD_DIM)
    tile_tokens = TILE_T * TILE_H * TILE_W
    tiles_t = NT // TILE_T
    tiles_h = NH // TILE_H
    tiles_w = NW // TILE_W
    count = tiles_t * tiles_h * tiles_w
    wide_count = HEADS // 4
    offsets = jnp.arange(3, dtype=jnp.int32) - 1
    limits = jnp.array([tiles_t, tiles_h, tiles_w], dtype=jnp.int32)
    is_wide = (lax.optimization_barrier(jnp.max(head_windows, axis=1)) > 1).astype(jnp.int32)
    wide_heads = jnp.argsort(-is_wide, stable=True)[:wide_count].astype(jnp.int32)
    wide_windows = head_windows[wide_heads]
    reach = jnp.abs(offsets)[None, None, :] <= (wide_windows // 2)[:, :, None]
    branch_outs = []
    text_outs = []
    for branch in range(2):
        query = video_query[branch]
        keys_all = video_key[branch]
        values_all = video_value[branch]
        keys_tiles = keys_all.reshape(tiles_t, TILE_T, tiles_h, TILE_H, tiles_w, TILE_W, F).transpose(0, 2, 4, 1, 3, 5, 6)
        values_tiles = values_all.reshape(tiles_t, TILE_T, tiles_h, TILE_H, tiles_w, TILE_W, F).transpose(0, 2, 4, 1, 3, 5, 6)
        text_valid = jnp.arange(L_TXT, dtype=jnp.int32) < text_count[branch]
        text_keys = text_key[branch].reshape(L_TXT, HEADS, HEAD_DIM)
        text_values = text_value[branch].reshape(L_TXT, HEADS, HEAD_DIM)

        def video_tile(index):
            tile_i = index // (tiles_h * tiles_w)
            tile_j = index // tiles_w % tiles_h
            tile_k = index % tiles_w
            start = (tile_i * TILE_T, tile_j * TILE_H, tile_k * TILE_W, jnp.int32(0))
            block = lax.dynamic_slice(query, start, (TILE_T, TILE_H, TILE_W, F)).reshape(tile_tokens, HEADS, HEAD_DIM).astype(jnp.float32)
            own_keys = keys_tiles[tile_i, tile_j, tile_k].reshape(tile_tokens, HEADS, HEAD_DIM)
            own_values = values_tiles[tile_i, tile_j, tile_k].reshape(tile_tokens, HEADS, HEAD_DIM)
            keys = jnp.concatenate((own_keys, text_keys), axis=0)
            values = jnp.concatenate((own_values, text_values), axis=0)
            valid = jnp.concatenate((jnp.ones((tile_tokens,), dtype=bool), text_valid))
            scores = jnp.einsum('qhd,khd->hqk', block, keys.astype(jnp.float32)) * inverse
            peak, total, acc = masked_partial(scores, valid[None, None, :], values)
            local = acc / total[..., None]
            place = jnp.stack((tile_i, tile_j, tile_k)).astype(jnp.int32)
            near = place[:, None] + offsets[None, :]
            inside = (near >= 0) & (near < limits[:, None])
            clamped = jnp.clip(near, 0, limits[:, None] - 1)
            region_keys = keys_tiles[clamped[0][:, None, None], clamped[1][None, :, None], clamped[2][None, None, :]].reshape(27 * tile_tokens, HEADS, HEAD_DIM)
            region_values = values_tiles[clamped[0][:, None, None], clamped[1][None, :, None], clamped[2][None, None, :]].reshape(27 * tile_tokens, HEADS, HEAD_DIM)
            wide_keys = jnp.concatenate((jnp.take(region_keys, wide_heads, axis=1), jnp.take(text_keys, wide_heads, axis=1)), axis=0)
            wide_values = jnp.concatenate((jnp.take(region_values, wide_heads, axis=1), jnp.take(text_values, wide_heads, axis=1)), axis=0)
            tile_ok = inside[None] & reach
            tile_ok = tile_ok[:, 0, :, None, None] & tile_ok[:, 1, None, :, None] & tile_ok[:, 2, None, None, :]
            wide_valid = jnp.concatenate((jnp.repeat(tile_ok.reshape(wide_count, 27), tile_tokens, axis=1), jnp.broadcast_to(text_valid[None, :], (wide_count, L_TXT))), axis=1)
            wide_scores = jnp.einsum('qhd,khd->hqk', jnp.take(block, wide_heads, axis=1), wide_keys.astype(jnp.float32)) * inverse
            wide_peak, wide_total, wide_acc = masked_partial(wide_scores, wide_valid[:, None, :], wide_values)
            result = local.at[wide_heads].set(wide_acc / wide_total[..., None])
            return result.astype(jnp.bfloat16)
        attended = lax.map(video_tile, jnp.arange(count, dtype=jnp.int32))
        attended = attended.transpose(0, 2, 1, 3).reshape(tiles_t, tiles_h, tiles_w, TILE_T, TILE_H, TILE_W, F)
        attended = attended.transpose(0, 3, 1, 4, 2, 5, 6).reshape(NT * NH * NW, F)
        text_queries = text_query[branch].reshape(L_TXT, HEADS, HEAD_DIM).astype(jnp.float32)

        def text_step(carry, index):
            tile_i = index // (tiles_h * tiles_w)
            tile_j = index // tiles_w % tiles_h
            tile_k = index % tiles_w
            start = (tile_i * TILE_T, tile_j * TILE_H, tile_k * TILE_W, jnp.int32(0))
            keys = lax.dynamic_slice(keys_all, start, (TILE_T, TILE_H, TILE_W, F)).reshape(tile_tokens, HEADS, HEAD_DIM)
            values = lax.dynamic_slice(values_all, start, (TILE_T, TILE_H, TILE_W, F)).reshape(tile_tokens, HEADS, HEAD_DIM)
            scores = jnp.einsum('lhd,khd->hlk', text_queries, keys.astype(jnp.float32)) * inverse
            return (combine_parts(carry, masked_partial(scores, True, values)), None)
        start_state = (jnp.full((HEADS, L_TXT), -jnp.inf, jnp.float32), jnp.zeros((HEADS, L_TXT), jnp.float32), jnp.zeros((HEADS, L_TXT, HEAD_DIM), jnp.float32))
        state, unused = lax.scan(text_step, start_state, jnp.arange(count, dtype=jnp.int32))
        text_scores = jnp.einsum('lhd,khd->hlk', text_queries, text_keys.astype(jnp.float32)) * inverse
        state = combine_parts(state, masked_partial(text_scores, text_valid[None, None, :], text_values))
        text_out = (state[2] / state[1][..., None]).transpose(1, 0, 2).reshape(L_TXT, F).astype(jnp.bfloat16)
        text_outs.append(text_out)
        projected = jnp.dot(attended, out_weight, preferred_element_type=jnp.float32)
        updated = hidden_state[branch].reshape(NT * NH * NW, D).astype(jnp.float32) + modulation[branch, 0] * projected
        mean = lax.optimization_barrier(jnp.mean(updated, axis=-1, keepdims=True))
        centered = updated - mean
        variance = lax.optimization_barrier(jnp.mean(centered * centered, axis=-1, keepdims=True))
        normed = centered * lax.rsqrt(variance + 1e-06) * (1.0 + modulation[branch, 2]) + modulation[branch, 1]
        branch_outs.append(jnp.dot(normed.astype(jnp.bfloat16), final_weight, preferred_element_type=jnp.float32))
    patches = branch_outs[1] + guidance[0] * (branch_outs[0] - branch_outs[1])
    return (patches.reshape(NT, NH, NW * OUT_CH), jnp.stack(text_outs))
```

```python
import functools
import math

import jax
import jax.numpy as jnp
from jax import lax
from jax.experimental import pallas as pl
from jax.experimental.pallas import tpu as pltpu
from jax.sharding import Mesh
from jax.sharding import PartitionSpec as P

DEPTH = 128
WIDE = 3
NEVER = -(2.0**100)
CHIPS = ("ta", "ha", "zh")
PLACES = 9
LOG2E = math.log2(math.e)
SCALE = LOG2E / math.sqrt(DEPTH)
MIB = 1024 * 1024

VMEM = pl.BlockSpec(memory_space=pltpu.VMEM)
SMEM = pl.BlockSpec(memory_space=pltpu.SMEM)
HBM = pl.BlockSpec(memory_space=pl.ANY)


def call(body, out_shape, in_specs, out_specs, scratch, flops, moved, *operands):
    return pl.pallas_call(
        body,
        grid=(1,),
        out_shape=out_shape,
        in_specs=in_specs,
        out_specs=out_specs,
        scratch_shapes=scratch,
        compiler_params=pltpu.CompilerParams(vmem_limit_bytes=56 * MIB),
        cost_estimate=pl.CostEstimate(flops=flops, bytes_accessed=moved, transcendentals=0),
    )(*operands)


def lanes(head):
    return pl.ds(pl.multiple_of(head * DEPTH, DEPTH), DEPTH)


def wide_heads(windows):
    found = jnp.int32(0)
    ids = [jnp.int32(0)] * WIDE
    for head in range(windows.shape[1]):
        wide = (windows[0, head] > 1) | (windows[1, head] > 1) | (windows[2, head] > 1)
        for at in range(WIDE):
            ids[at] = jnp.where(wide & (found == at), head, ids[at])
        found = found + wide.astype(jnp.int32)
    return ids


def outer(a, b):
    return lax.dot_general(a, b, (((1,), (1,)), ((), ())), preferred_element_type=jnp.float32)


def inner(a, b):
    return jnp.dot(a, b, preferred_element_type=jnp.float32)


def low(x):
    return x.astype(jnp.bfloat16)


def high(x):
    return x.astype(jnp.float32)


def pack_body(windows, query, key, value, pairs, queries, held, sems):
    ids = wide_heads(windows)
    copies = []
    for at in range(WIDE):
        copies.append(pltpu.make_async_copy(key.at[:, lanes(ids[at])], pairs.at[at], sems.at[at]))
        copies.append(
            pltpu.make_async_copy(
                value.at[:, lanes(ids[at])], pairs.at[WIDE + at], sems.at[WIDE + at]
            )
        )
    asked = [
        pltpu.make_async_copy(query.at[:, lanes(ids[at])], held.at[at], sems.at[2 * WIDE + at])
        for at in range(WIDE)
    ]
    for copy in copies + asked:
        copy.start()
    for at in range(WIDE):
        asked[at].wait()
        queries[at] = held[at].T
    for copy in copies:
        copy.wait()


def quarter_body(weight, after, out, sem):
    rows = out.shape[0]
    first = pl.multiple_of(lax.axis_index("co") * rows, rows)
    copy = pltpu.make_async_copy(weight.at[pl.ds(first, rows), :], out, sem)
    copy.start()
    copy.wait()


def text_partial(query, key, value, rows, head, before, rounded):
    cols = slice(head * DEPTH, (head + 1) * DEPTH)
    scores = outer(query[rows, cols], key[:, cols]) * SCALE
    peak = jnp.max(scores, axis=1, keepdims=True)
    if before is not None:
        peak = jnp.maximum(peak, before[0])
    weights = jnp.exp2(scores - peak)
    total = jnp.sum(weights, axis=1, keepdims=True)
    mixed = inner(low(weights), value[:, cols])
    if before is not None:
        factor = jnp.exp2(before[0] - peak)
        total = total + before[1] * factor
        mixed = mixed + before[2] * factor
    if rounded:
        top = high(low(peak))
        factor = jnp.exp2(peak - top)
        peak, total, mixed = top, total * factor, mixed * factor
    return peak, total, mixed


def text_far_body(query, key, value, sums, stats):
    half = sums.shape[0]
    rows = pl.ds(pl.multiple_of((1 - lax.axis_index("co")) * half, half), half)
    lane = lax.broadcasted_iota(jnp.int32, stats.shape, 1)
    held = jnp.zeros(stats.shape, jnp.float32)
    heads = query.shape[1] // DEPTH
    for head in range(heads):
        peak, total, mixed = text_partial(query, key, value, rows, head, None, False)
        sums[:, head * DEPTH : (head + 1) * DEPTH] = mixed
        held = jnp.where(lane == head, peak, jnp.where(lane == 16 + head, total, held))
    stats[...] = held


def text_own_body(query, key, value, sums, stats, text_key, text_value, out):
    half = sums.shape[0]
    width = query.shape[1]
    heads = width // DEPTH
    rows = pl.ds(pl.multiple_of(lax.axis_index("co") * half, half), half)
    lane = lax.broadcasted_iota(jnp.int32, stats.shape, 1)
    held = jnp.zeros(stats.shape, jnp.float32)
    for head in range(heads):
        cols = slice(head * DEPTH, (head + 1) * DEPTH)
        before = (stats[:, head : head + 1], stats[:, 16 + head : 17 + head], sums[:, cols])
        peak, total, mixed = text_partial(query, key, value, rows, head, before, True)
        coarse = low(mixed)
        out[:, cols] = coarse
        out[:, width + head * DEPTH : width + (head + 1) * DEPTH] = low(mixed - high(coarse))
        big = high(low(total))
        held = jnp.where(lane == head, peak, held)
        held = jnp.where(lane == 16 + head, big, held)
        held = jnp.where(lane == 32 + head, total - big, held)
    out[:, 2 * width : 3 * width] = low(jnp.broadcast_to(high(text_key[...]), (half, width)))
    out[:, 3 * width : 4 * width] = low(jnp.broadcast_to(high(text_value[...]), (half, width)))
    out[:, 4 * width :] = low(held)


def text_masks(count, rows, cols):
    place = 2 * lax.broadcasted_iota(jnp.int32, (rows, cols), 0)
    core = lax.axis_index("co")
    return place + core < count, place + 1 - core < count


def narrow_body(windows, count, query, key, value, tk0, tv0, tk1, tv1, out, ids):
    heads = windows.shape[1]
    found = jnp.int32(0)
    for head in range(heads):
        wide = (windows[0, head] > 1) | (windows[1, head] > 1) | (windows[2, head] > 1)
        ids[jnp.where(wide, heads, found)] = head
        found = found + 1 - wide.astype(jnp.int32)
    tokens = query.shape[0]
    near, far = text_masks(count[0], tk0.shape[0], tokens)

    def step(group, carry):
        for at in range(3):
            cols = lanes(ids[group * 3 + at])
            asked = query[:, cols].T
            scores = inner(key[:, cols], asked) * SCALE
            first = jnp.where(near, inner(tk0[:, cols], asked) * SCALE, NEVER)
            second = jnp.where(far, inner(tk1[:, cols], asked) * SCALE, NEVER)
            peak = jnp.maximum(
                jnp.max(scores, axis=0, keepdims=True),
                jnp.max(jnp.maximum(first, second), axis=0, keepdims=True),
            )
            scores = jnp.exp2(scores - peak)
            first = jnp.exp2(first - peak)
            second = jnp.exp2(second - peak)
            total = jnp.sum(scores, axis=0, keepdims=True) + jnp.sum(
                first + second, axis=0, keepdims=True
            )
            mixed = (
                inner(value[:, cols].T, low(scores))
                + inner(tv0[:, cols].T, low(first))
                + inner(tv1[:, cols].T, low(second))
            )
            out[:, cols] = low((mixed / total).T)
        return carry

    lax.fori_loop(0, (heads - WIDE) // 3, step, 0)


def place_ok(windows, head, at, needs_time):
    row_at, zone, core = lax.axis_index("ha"), lax.axis_index("zh"), lax.axis_index("co")
    a, c = at // 3, at % 3
    rows = windows[1, head] > 1
    cols = windows[2, head] > 1
    row_in = (a == 0) | (
        rows & (((a == 1) & (row_at > 0)) | ((a == 2) & (row_at < lax.axis_size("ha") - 1)))
    )
    outer_in = jnp.where(core == 0, zone > 0, zone < lax.axis_size("zh") - 1)
    col_in = (c == 0) | (cols & ((c == 2) | outer_in))
    ok = row_in & col_in
    if needs_time:
        ok = ok & (windows[0, head] > 1)
    return ok


def wide_tiles(windows, ids, sources, keys, values, sems, needs_time):
    own, left, right, inside = sources
    for at in range(WIDE):
        for place in range(PLACES):
            a, c = divmod(place, 3)
            source = inside.at[a] if c == 2 else (own, left, right)[a].at[c]
            slot = at * PLACES + place

            @pl.when(place_ok(windows, ids[at], jnp.int32(place), needs_time))
            def _(source=source, slot=slot, at=at):
                pltpu.make_async_copy(source.at[at], keys.at[slot], sems.at[slot, 0]).start()
                pltpu.make_async_copy(source.at[WIDE + at], values.at[slot], sems.at[slot, 1]).start()


def wide_head(windows, ids, at, sources, keys, values, sems, needs_time, asked, peak, total, mixed):
    own = sources[0]

    def step(place, carry):
        @pl.when(place_ok(windows, ids[at], place, needs_time))
        def _():
            slot = at * PLACES + place
            pltpu.make_async_copy(own.at[0, 0], keys.at[slot], sems.at[slot, 0]).wait()
            pltpu.make_async_copy(own.at[0, 0], values.at[slot], sems.at[slot, 1]).wait()
            key = keys[slot]
            value = values[slot].T
            for part, query in enumerate(asked):
                scores = inner(key, query) * SCALE
                top = jnp.maximum(peak[part], jnp.max(scores, axis=0, keepdims=True))
                factor = jnp.exp2(peak[part] - top)
                weights = jnp.exp2(scores - top)
                total[part] = total[part] * factor + jnp.sum(weights, axis=0, keepdims=True)
                mixed[part] = mixed[part] * factor + inner(value, low(weights))
                peak[part] = top

        return carry

    lax.fori_loop(0, PLACES, step, 0)


def wide_lent_body(
    windows, own, left, right, inside, before, after, out0, out1, keys, values, peak, total, mixed, sems
):
    ids = wide_heads(windows)
    sources = (own, left, right, inside)
    wide_tiles(windows, ids, sources, keys, values, sems, True)
    for at in range(WIDE):
        peak[...] = jnp.full(peak.shape, NEVER, jnp.float32)
        total[...] = jnp.zeros(total.shape, jnp.float32)
        mixed[...] = jnp.zeros(mixed.shape, jnp.float32)
        asked = (before[at], after[at])
        wide_head(windows, ids, at, sources, keys, values, sems, True, asked, peak, total, mixed)
        for part, out in enumerate((out0, out1)):
            top = high(low(peak[part]))
            factor = jnp.exp2(peak[part] - top)
            sums = total[part] * factor
            big = high(low(sums))
            row = lax.broadcasted_iota(jnp.int32, (16, sums.shape[1]), 0)
            held = jnp.where(row == 0, top, jnp.where(row == 1, big, sums - big))
            out[at, :DEPTH] = low(mixed[part] * factor)
            out[at, DEPTH:] = low(held)


def wide_own_body(
    windows, count, own, left, right, inside, queries, tk0, tv0, tk1, tv1,
    sums, stats, keys, values, peak, total, mixed, sems,
):
    ids = wide_heads(windows)
    sources = (own, left, right, inside)
    wide_tiles(windows, ids, sources, keys, values, sems, False)
    near, far = text_masks(count[0], tk0.shape[0], queries.shape[2])
    for at in range(WIDE):
        cols = lanes(ids[at])
        asked = queries[at]
        first = jnp.where(near, inner(tk0[:, cols], asked) * SCALE, NEVER)
        second = jnp.where(far, inner(tk1[:, cols], asked) * SCALE, NEVER)
        top = jnp.max(jnp.maximum(first, second), axis=0, keepdims=True)
        first = jnp.exp2(first - top)
        second = jnp.exp2(second - top)
        peak[0] = top
        total[0] = jnp.sum(first + second, axis=0, keepdims=True)
        mixed[0] = inner(tv0[:, cols].T, low(first)) + inner(tv1[:, cols].T, low(second))
        wide_head(windows, ids, at, sources, keys, values, sems, False, (asked,), peak, total, mixed)
        row = lax.broadcasted_iota(jnp.int32, stats.shape[1:], 0)
        stats[at] = jnp.where(row == 0, peak[0], total[0])
        sums[at] = mixed[0]


def text_merge_body(query, count, got, tk1, tv1, out):
    width = query.shape[1]
    core = lax.axis_index("co")
    chip = (
        lax.axis_index("ta") * lax.axis_size("ha") + lax.axis_index("ha")
    ) * lax.axis_size("zh") + lax.axis_index("zh")
    sources = got.shape[0]
    at = core * sources + chip
    block = high(query[pl.ds(pl.multiple_of(at // 16 * 16, 16), 16), :])
    row = lax.broadcasted_iota(jnp.int32, block.shape, 0)
    asked = jnp.sum(jnp.where(row == at % 16, block, 0.0), axis=0, keepdims=True)
    near, far = text_masks(count[0], sources, 1)
    stats = high(got[:, 4 * width :])
    for head in range(width // DEPTH):
        cols = slice(head * DEPTH, (head + 1) * DEPTH)

        def part(block, head=head):
            return high(got[:, block * width + head * DEPTH : block * width + (head + 1) * DEPTH])

        peak = stats[:, head : head + 1]
        total = stats[:, 16 + head : 17 + head] + stats[:, 32 + head : 33 + head]
        mine = asked[:, cols]
        first = jnp.sum(part(2) * mine, axis=1, keepdims=True) * SCALE
        second = jnp.sum(high(tk1[:, cols]) * mine, axis=1, keepdims=True) * SCALE
        first = jnp.where(near, first, NEVER)
        second = jnp.where(far, second, NEVER)
        top = jnp.max(jnp.maximum(peak, jnp.maximum(first, second)), axis=0, keepdims=True)
        factor = jnp.exp2(peak - top)
        first = jnp.exp2(first - top)
        second = jnp.exp2(second - top)
        whole = jnp.sum(factor * total + first + second, axis=0, keepdims=True)
        mixed = jnp.sum(
            factor * (part(0) + part(1)) + first * part(3) + second * high(tv1[:, cols]),
            axis=0,
            keepdims=True,
        )
        out[:, cols] = low(jnp.broadcast_to(mixed / whole, (sources, DEPTH)))


def final_body(
    windows, sums, stats, back0, back1, narrow, w_own, w_mine, w_other, hidden, modulation, final, out,
    attended, weight, updated, sems, *, parts,
):
    ids = wide_heads(windows)
    branch, core = lax.axis_index("cfg"), lax.axis_index("co")
    half, model = w_own.shape
    part_cols = model // parts
    copies = []
    for part in range(parts):
        cols = pl.ds(part * part_cols, part_cols)
        for at, (source, row) in enumerate(
            (
                (w_own, branch * half),
                (w_mine, (1 - branch) * half + core * (half // 2)),
                (w_other, (1 - branch) * half + (1 - core) * (half // 2)),
            )
        ):
            rows = pl.ds(pl.multiple_of(row, half // 2), source.shape[0])
            copies.append(
                pltpu.make_async_copy(
                    source.at[:, cols], weight.at[rows, cols], sems.at[part, at]
                )
            )
    for copy in copies:
        copy.start()
    attended[...] = narrow[...]
    time_at = lax.axis_index("ta")
    inside = (time_at > 0, time_at < lax.axis_size("ta") - 1)
    for at in range(WIDE):
        peaks = [stats[at, 0:1]]
        totals = [stats[at, 1:2]]
        for back, ok in zip((back0, back1), inside):
            rows = high(back[at, DEPTH:])
            peaks.append(jnp.where(ok, rows[0:1], NEVER))
            totals.append(jnp.where(ok, rows[1:2] + rows[2:3], 0.0))
        top = jnp.maximum(peaks[0], jnp.maximum(peaks[1], peaks[2]))
        factors = [jnp.exp2(peak - top) for peak in peaks]
        total = sum(factor * whole for factor, whole in zip(factors, totals))
        mixed = (
            sums[at] * factors[0]
            + high(back0[at, :DEPTH]) * factors[1]
            + high(back1[at, :DEPTH]) * factors[2]
        )
        attended[:, lanes(ids[at])] = low((mixed / total).T)
    tokens = attended.shape[0]
    running = jnp.zeros((tokens, 1), jnp.float32)
    for part in range(parts):
        cols = slice(part * part_cols, (part + 1) * part_cols)
        for copy in copies[3 * part : 3 * part + 3]:
            copy.wait()
        projected = inner(attended[...], weight[:, cols])
        fresh = high(hidden[:, cols]) + modulation[0, :, cols] * projected
        updated[:, cols] = fresh
        running = running + jnp.sum(fresh, axis=1, keepdims=True)
    mean = running / model
    spread = jnp.zeros((tokens, 1), jnp.float32)
    for part in range(parts):
        cols = slice(part * part_cols, (part + 1) * part_cols)
        centered = updated[:, cols] - mean
        spread = spread + jnp.sum(centered * centered, axis=1, keepdims=True)
    factor = lax.rsqrt(spread / model + 1e-06)
    result = jnp.zeros(out.shape, jnp.float32)
    for part in range(parts):
        cols = slice(part * part_cols, (part + 1) * part_cols)
        normed = (updated[:, cols] - mean) * factor * (1.0 + modulation[2, :, cols])
        normed = normed + modulation[1, :, cols]
        result = result + outer(low(normed), final[:, cols])
    out[...] = result


def shift(x, axis, step):
    size = lax.axis_size(axis)
    return lax.ppermute(x, axis, [(i, i + step) for i in range(size) if 0 <= i + step < size])


def swap_core(x):
    return lax.ppermute(x, "co", [(0, 1), (1, 0)])


def local(
    video_query, video_key, video_value, text_query, text_key, text_value, text_count, head_windows,
    hidden_state, out_weight, final_weight, modulation, guidance,
):
    frames, rows, cols, width = video_query.shape[1:]
    tokens = frames * rows * cols
    heads = head_windows.shape[0]
    text_len = text_query.shape[1]
    half_text = text_len // 2
    model = out_weight.shape[1]
    half_width = out_weight.shape[0]
    bf16, f32 = jnp.bfloat16, jnp.float32
    shape = jax.ShapeDtypeStruct
    query = video_query.reshape(tokens, width)
    key = video_key.reshape(tokens, width)
    value = video_value.reshape(tokens, width)
    text_query = text_query[0]
    windows = head_windows.T
    core = lax.axis_index("co")
    branch = lax.axis_index("cfg")
    zones = lax.axis_size("zh")

    pairs, queries = call(
        pack_body,
        (shape((2 * WIDE, tokens, DEPTH), bf16), shape((WIDE, DEPTH, tokens), bf16)),
        [SMEM, HBM, HBM, HBM],
        (VMEM, VMEM),
        [pltpu.VMEM((WIDE, tokens, DEPTH), bf16), pltpu.SemaphoreType.DMA((3 * WIDE,))],
        0, 4 * 1024 * 1024,
        windows, query, key, value,
    )
    beside = [(2 * z + 1, 2 * z + 2) for z in range(zones - 1)]
    beside = beside + [(b, a) for a, b in beside]
    next_pairs = lax.ppermute(pairs, ("zh", "co"), beside)
    from_before = shift(queries, "ta", 1)
    from_after = shift(queries, "ta", -1)

    def at(branch_at, zone, core_at):
        return (branch_at * zones + zone) * 2 + core_at

    weight_pairs = []
    for z in range(zones):
        weight_pairs.append((at(0, z, 0), at(1, z, 0)))
        weight_pairs.append((at(0, (z + 1) % zones, 1), at(1, z, 1)))
    weight_pairs = weight_pairs + [(b, a) for a, b in weight_pairs]
    quarter = call(
        quarter_body,
        shape((half_width // 2, model), bf16),
        [HBM, HBM], VMEM, [pltpu.SemaphoreType.DMA], 0, 2 * half_width * model,
        out_weight, next_pairs,
    )
    w_mine = lax.ppermute(quarter, ("cfg", "zh", "co"), weight_pairs)

    text_flops = 2 * 2 * half_text * tokens * width
    text_bytes = 2 * 2 * tokens * width
    far_sums, far_stats = call(
        text_far_body,
        (shape((half_text, width), f32), shape((half_text, DEPTH), f32)),
        [VMEM] * 3, (VMEM, VMEM), [], text_flops, text_bytes,
        text_query, key, value,
    )
    payload = call(
        text_own_body,
        shape((half_text, 4 * width + DEPTH), bf16),
        [VMEM] * 7, VMEM, [], text_flops, text_bytes,
        text_query, key, value, swap_core(far_sums), swap_core(far_stats), text_key[0], text_value[0],
    )
    got = lax.all_to_all(payload, CHIPS, 0, 0, tiled=True)

    own = jnp.stack((pairs, next_pairs))
    left = shift(own, "ha", 1)
    right = shift(own, "ha", -1)
    inside = swap_core(jnp.stack((pairs, left[0], right[0])))
    w_other = swap_core(w_mine)

    got_other = swap_core(got)

    def text_block(index):
        return pl.BlockSpec((half_text, width), lambda step: (0, index))

    text_specs = [text_block(2), text_block(3), text_block(2), text_block(3)]
    narrow = call(
        narrow_body,
        shape((tokens, width), bf16),
        [SMEM, SMEM, VMEM, VMEM, VMEM] + text_specs, VMEM,
        [pltpu.SMEM((heads + 1,), jnp.int32)],
        4 * (heads - WIDE) * tokens * (tokens + text_len) * DEPTH, 5 * tokens * width * 2,
        windows, text_count, query, key, value, got, got, got_other, got_other,
    )

    def wide_scratch(parts):
        return [
            pltpu.VMEM((WIDE * PLACES, tokens, DEPTH), bf16),
            pltpu.VMEM((WIDE * PLACES, tokens, DEPTH), bf16),
            pltpu.VMEM((parts, 1, tokens), f32),
            pltpu.VMEM((parts, 1, tokens), f32),
            pltpu.VMEM((parts, DEPTH, tokens), f32),
            pltpu.SemaphoreType.DMA((WIDE * PLACES, 2)),
        ]

    tile_flops = 4 * tokens * tokens * DEPTH
    lent = shape((WIDE, DEPTH + 16, tokens), bf16)
    to_before, to_after = call(
        wide_lent_body,
        (lent, lent),
        [SMEM, HBM, HBM, HBM, HBM, VMEM, VMEM], (VMEM, VMEM),
        wide_scratch(2), 2 * WIDE * PLACES * tile_flops, 6 * MIB,
        windows, own, left, right, inside, from_before, from_after,
    )
    back_after = shift(to_before, "ta", -1)
    back_before = shift(to_after, "ta", 1)
    sums, stats = call(
        wide_own_body,
        (shape((WIDE, DEPTH, tokens), f32), shape((WIDE, 8, tokens), f32)),
        [SMEM, SMEM, HBM, HBM, HBM, HBM, VMEM] + text_specs, (VMEM, VMEM),
        wide_scratch(1), WIDE * PLACES * tile_flops, 6 * MIB,
        windows, text_count, own, left, right, inside, queries, got, got, got_other, got_other,
    )

    finished = call(
        text_merge_body,
        shape((half_text, width), bf16),
        [VMEM, SMEM, VMEM] + text_specs[2:], VMEM, [], 0, 2 * MIB,
        text_query, text_count, got, got_other, got_other,
    )
    text_mine = lax.all_to_all(finished, CHIPS, 0, 0, tiled=True)
    text_other = swap_core(text_mine)
    text_out = jnp.where(
        core == 0,
        jnp.concatenate((text_mine, text_other)),
        jnp.concatenate((text_other, text_mine)),
    )

    parts = 6
    branch_out = call(
        functools.partial(final_body, parts=parts),
        shape((tokens, final_weight.shape[1]), f32),
        [SMEM, VMEM, VMEM, VMEM, VMEM, VMEM, HBM, HBM, HBM, VMEM, VMEM, VMEM], VMEM,
        [
            pltpu.VMEM((tokens, width), bf16),
            pltpu.VMEM((width, model), bf16),
            pltpu.VMEM((tokens, model), f32),
            pltpu.SemaphoreType.DMA((parts, 3)),
        ],
        2 * tokens * width * model, 16 * MIB,
        windows, sums, stats, back_before, back_after, narrow, out_weight, w_mine, w_other,
        hidden_state.reshape(tokens, model), modulation.transpose(1, 0, 2), final_weight.T,
    )
    half_rows = rows // 2
    grid = branch_out.reshape(frames, rows, cols * final_weight.shape[1])
    kept = lax.dynamic_slice_in_dim(grid, branch * half_rows, half_rows, 1)
    sent = lax.dynamic_slice_in_dim(grid, (1 - branch) * half_rows, half_rows, 1)
    received = lax.ppermute(sent, "cfg", [(0, 1), (1, 0)])
    conditional = jnp.where(branch == 0, kept, received)
    unconditional = jnp.where(branch == 0, received, kept)
    guided = unconditional + guidance[0] * (conditional - unconditional)
    return (guided, text_out[None])


def solution(mesh):
    devices = mesh.devices.reshape(mesh.devices.shape[:3] + (mesh.devices.shape[3] // 2, 2))
    split = Mesh(devices, ("cfg", "ta", "ha", "zh", "co"))
    wa = ("zh", "co")
    everyone = ("ta", "ha", "zh", "co")
    video = P("cfg", "ta", "ha", wa, None)
    in_specs = (
        video, video, video,
        P("cfg", None, None),
        P("cfg", everyone, None),
        P("cfg", everyone, None),
        P("cfg"),
        P(),
        video,
        P("cfg", None),
        P(),
        P("cfg", None, None),
        P(),
    )
    out_specs = (P("ta", ("ha", "cfg"), wa), P("cfg", None, None))
    return jax.shard_map(local, mesh=split, in_specs=in_specs, out_specs=out_specs, check_vma=False)
```

```python
import functools
import math

import jax
import jax.numpy as jnp
from jax import lax
from jax.experimental import pallas as pl
from jax.experimental.pallas import tpu as pltpu
from jax.sharding import Mesh
from jax.sharding import PartitionSpec as P

DEPTH = 128
WIDE = 3
NEVER = -(2.0**100)
CHIPS = ("ta", "ha", "zh")
SLOTS = 40
ENDS = 16
LOG2E = math.log2(math.e)
SCALE = LOG2E / math.sqrt(DEPTH)
MIB = 1024 * 1024

VMEM = pl.BlockSpec(memory_space=pltpu.VMEM)
SMEM = pl.BlockSpec(memory_space=pltpu.SMEM)
HBM = pl.BlockSpec(memory_space=pl.ANY)


def call(body, out_shape, in_specs, out_specs, scratch, vmem, flops, moved, *operands):
    return pl.pallas_call(
        body,
        grid=(1,),
        out_shape=out_shape,
        in_specs=in_specs,
        out_specs=out_specs,
        scratch_shapes=scratch,
        compiler_params=pltpu.CompilerParams(vmem_limit_bytes=64 * MIB - 65536),
        cost_estimate=pl.CostEstimate(flops=flops, bytes_accessed=moved, transcendentals=0),
    )(*operands)


def lanes(head):
    return pl.ds(pl.multiple_of(head * DEPTH, DEPTH), DEPTH)


def wide_heads(windows):
    found = jnp.int32(0)
    ids = [jnp.int32(0)] * WIDE
    for head in range(windows.shape[1]):
        wide = (windows[0, head] > 1) | (windows[1, head] > 1) | (windows[2, head] > 1)
        for at in range(WIDE):
            ids[at] = jnp.where(wide & (found == at), head, ids[at])
        found = found + wide.astype(jnp.int32)
    return ids


def outer(a, b):
    return lax.dot_general(a, b, (((1,), (1,)), ((), ())), preferred_element_type=jnp.float32)


def inner(a, b):
    return jnp.dot(a, b, preferred_element_type=jnp.float32)


def low(x):
    return x.astype(jnp.bfloat16)


def high(x):
    return x.astype(jnp.float32)


def slot(index):
    return pl.ds(index, 64, stride=SLOTS), slice(None)


def after_body(*refs):
    pass


def after(x, *others):
    return pl.pallas_call(
        after_body,
        out_shape=jax.ShapeDtypeStruct(x.shape, x.dtype),
        in_specs=[HBM] * (1 + len(others)),
        out_specs=HBM,
        input_output_aliases={0: 0},
    )(x, *others)


def pack_body(windows, query, key, value, pairs, queries, held, sems):
    ids = wide_heads(windows)
    tokens = query.shape[0]
    copies = []
    for at in range(WIDE):
        cols = lanes(ids[at])
        copies.append(pltpu.make_async_copy(query.at[:, cols], held.at[at], sems.at[at]))
        copies.append(
            pltpu.make_async_copy(value.at[:, cols], held.at[WIDE + at], sems.at[WIDE + at])
        )
        copies.append(pltpu.make_async_copy(key.at[:, cols], pairs.at[at], sems.at[2 * WIDE + at]))
    for copy in copies:
        copy.start()
    for copy in copies:
        copy.wait()
    for at in range(WIDE):
        queries[at] = held[at].T
        for row in range(0, tokens, DEPTH):
            pairs[WIDE + at, row : row + DEPTH] = held[WIDE + at, row : row + DEPTH].T


def quarter_body(weight, after, out, held, sems):
    rows = out.shape[0]
    first = lax.axis_index("co") * rows
    chunk = rows // 4
    loads = []
    stores = []
    for at in range(4):
        source = pl.ds(pl.multiple_of(first + at * chunk, chunk), chunk)
        here = pl.ds(at * chunk, chunk)
        loads.append(pltpu.make_async_copy(weight.at[source, :], held.at[here], sems.at[0, at]))
        stores.append(pltpu.make_async_copy(held.at[here], out.at[here], sems.at[1, at]))
    for load in loads:
        load.start()
    for load, store in zip(loads, stores):
        load.wait()
        store.start()
    for store in stores:
        store.wait()


def text_video_body(query, key, value, after, own_sums, far_sums, own_stats, far_stats, held):
    half = own_sums.shape[0]
    core = lax.axis_index("co")
    own_rows = pl.ds(pl.multiple_of(core * half, half), half)
    far_rows = pl.ds(pl.multiple_of((1 - core) * half, half), half)
    held[...] = jnp.zeros(held.shape, jnp.float32)
    for head in range(query.shape[1] // DEPTH):
        cols = slice(head * DEPTH, (head + 1) * DEPTH)
        asked = jnp.concatenate((query[own_rows, cols], query[far_rows, cols]), axis=0).T
        scores = inner(key[:, cols], asked) * SCALE
        peak = jnp.max(scores, axis=0, keepdims=True)
        weights = jnp.exp2(scores - peak)
        held[head : head + 1] = peak
        held[16 + head : 17 + head] = jnp.sum(weights, axis=0, keepdims=True)
        mixed = inner(low(weights).T, value[:, cols])
        own_sums[:, cols] = mixed[:half]
        far_sums[:, cols] = mixed[half:]
    stats = held[...].T
    own_stats[...] = stats[:half]
    far_stats[...] = stats[half:]


def text_join_body(sums, stats, far_sums, far_stats, text_key, text_value, *rest):
    out = rest[-1]
    half, width = sums.shape
    heads = width // DEPTH
    lane = lax.broadcasted_iota(jnp.int32, stats.shape, 1)
    held = jnp.zeros(stats.shape, jnp.float32)
    for head in range(heads):
        cols = slice(head * DEPTH, (head + 1) * DEPTH)
        first, second = stats[:, head : head + 1], far_stats[:, head : head + 1]
        top = jnp.maximum(first, second)
        first, second = jnp.exp2(first - top), jnp.exp2(second - top)
        total = stats[:, 16 + head : 17 + head] * first + far_stats[:, 16 + head : 17 + head] * second
        out[slot(head)] = sums[:, cols] * first + far_sums[:, cols] * second
        held = jnp.where(lane == head, top, jnp.where(lane == 16 + head, total, held))
        out[slot(heads + 1 + head)] = jnp.broadcast_to(high(text_key[:, cols]), (half, DEPTH))
        out[slot(2 * heads + 1 + head)] = jnp.broadcast_to(high(text_value[:, cols]), (half, DEPTH))
    out[slot(heads)] = held


def text_masks(count, rows, cols):
    place = 2 * lax.broadcasted_iota(jnp.int32, (rows, cols), 0)
    core = lax.axis_index("co")
    return place + core < count, place + 1 - core < count


def narrow_body(
    windows, count, query, key, value, queries, got, got_other, finished, out, sums, stats,
    text_keys, text_values, ids,
):
    heads = windows.shape[1]
    half = got.shape[0] // SLOTS
    for head in range(heads):
        for at, source in enumerate((got, got_other)):
            rows = slice(at * half, (at + 1) * half)
            text_keys[head, rows] = low(source[slot(heads + 1 + head)])
            text_values[head, rows] = low(source[slot(2 * heads + 1 + head)])
    found = jnp.int32(0)
    for head in range(heads):
        wide = (windows[0, head] > 1) | (windows[1, head] > 1) | (windows[2, head] > 1)
        ids[jnp.where(wide, heads, found)] = head
        found = found + 1 - wide.astype(jnp.int32)
    tokens = query.shape[0]
    valid = jnp.concatenate(
        [high(mask.astype(jnp.int32)) for mask in text_masks(count[0], half, DEPTH)], axis=0
    ) > 0.5

    def step(group, carry):
        for at in range(3):
            head = ids[group * 3 + at]
            cols = lanes(head)
            keys = jnp.concatenate((key[:, cols], text_keys[head]), axis=0)
            values = jnp.concatenate((value[:, cols], text_values[head]), axis=0).T
            asked = query[:, cols].T
            for first in range(0, tokens, DEPTH):
                scores = inner(keys, asked[:, first : first + DEPTH]) * SCALE
                near, text = scores[:tokens], jnp.where(valid, scores[tokens:], NEVER)
                peak = jnp.maximum(
                    jnp.max(near, axis=0, keepdims=True), jnp.max(text, axis=0, keepdims=True)
                )
                weights = jnp.exp2(jnp.concatenate((near, text), axis=0) - peak)
                total = jnp.sum(weights, axis=0, keepdims=True)
                mixed = inner(values, low(weights))
                out[first : first + DEPTH, cols] = low((mixed / total).T)
        return carry

    lax.fori_loop(0, (heads - WIDE) // 3, step, 0)
    row = lax.broadcasted_iota(jnp.int32, (stats.shape[1], DEPTH), 0)
    for at, head in enumerate(wide_heads(windows)):
        keys = text_keys[head]
        values = text_values[head].T
        for first in range(0, tokens, DEPTH):
            some = slice(first, first + DEPTH)
            scores = jnp.where(valid, inner(keys, queries[at, :, some]) * SCALE, NEVER)
            peak = jnp.max(scores, axis=0, keepdims=True)
            weights = jnp.exp2(scores - peak)
            stats[at, :, some] = jnp.where(row == 0, peak, jnp.sum(weights, axis=0, keepdims=True))
            sums[at, :, some] = inner(values, low(weights))


def place_ok(windows, head, a, c):
    row_at, zone, core = lax.axis_index("ha"), lax.axis_index("zh"), lax.axis_index("co")
    ok = jnp.bool_(True)
    if a > 0:
        ok = windows[1, head] > 1
        ok = ok & ((row_at > 0) if a == 1 else (row_at < lax.axis_size("ha") - 1))
    if c > 0:
        ok = ok & (windows[2, head] > 1)
    if c == 1:
        ok = ok & jnp.where(core == 0, zone > 0, zone < lax.axis_size("zh") - 1)
    return ok


def wide_walk(
    windows, tables, asked, before, keys, values, peak, total, mixed, counts, sems, finish
):
    ids = wide_heads(windows)
    tokens = asked[0].shape[2]
    places = list(tables)
    for at in range(WIDE):
        found = jnp.int32(0)
        for number, (a, c) in enumerate(places):
            source = tables[a, c]
            ok = place_ok(windows, ids[at], a, c)
            slot_at = at * len(places) + number
            rows = pl.ds(pl.multiple_of(found * tokens, tokens), tokens)

            @pl.when(ok)
            def _(source=source, slot_at=slot_at, rows=rows, at=at):
                pltpu.make_async_copy(source.at[at], keys.at[at, rows], sems.at[slot_at, 0]).start()
                pltpu.make_async_copy(
                    source.at[WIDE + at], values.at[at, rows], sems.at[slot_at, 1]
                ).start()

            found = found + ok.astype(jnp.int32)
        counts[at] = found
        counts[WIDE + at] = ids[at]
    any_tile = tables[places[0]]

    def head_step(at, carry):
        head = counts[WIDE + at]
        count = counts[at]
        for number, (a, c) in enumerate(places):

            @pl.when(place_ok(windows, head, a, c))
            def _(number=number):
                slot_at = at * len(places) + number
                whole = pl.ds(0, tokens)
                pltpu.make_async_copy(any_tile.at[0], keys.at[at, whole], sems.at[slot_at, 0]).wait()
                pltpu.make_async_copy(any_tile.at[0], values.at[at, whole], sems.at[slot_at, 1]).wait()

        before(at)

        def span(start, size, sources):
            rows = pl.ds(pl.multiple_of(start, tokens), size)
            key = keys[at, rows]
            value = values[at, rows]
            value = jnp.concatenate(
                [value[row : row + DEPTH] for row in range(0, size, DEPTH)], axis=1
            )
            for part, source in sources:
                for first in range(0, tokens, DEPTH):
                    some = slice(part * tokens + first, part * tokens + first + DEPTH)
                    scores = inner(key, source[at, :, first : first + DEPTH]) * SCALE
                    held = peak[:, some]
                    top = jnp.maximum(held, jnp.max(scores, axis=0, keepdims=True))
                    factor = jnp.exp2(held - top)
                    weights = jnp.exp2(scores - top)
                    total[:, some] = total[:, some] * factor + jnp.sum(
                        weights, axis=0, keepdims=True
                    )
                    mixed[:, some] = mixed[:, some] * factor + inner(value, low(weights))
                    peak[:, some] = top

        def spans(sources):
            @pl.when(count == len(places))
            def _():
                span(0, len(places) * tokens, sources)

            @pl.when(count < len(places))
            def _():
                threes = count // 3 if len(places) > 3 else 0

                def three(step, carry):
                    span(step * 3 * tokens, 3 * tokens, sources)
                    return carry

                def one(step, carry):
                    span(step * tokens, tokens, sources)
                    return carry

                if len(places) > 3:
                    lax.fori_loop(0, threes, three, 0)
                lax.fori_loop(threes * 3, count, one, 0)

        spans(((0, asked[0]),))

        @pl.when(windows[0, head] > 1)
        def _():
            spans(((1, asked[1]), (2, asked[2])))

        finish(at)
        return carry

    lax.fori_loop(0, WIDE, head_step, 0)


def wide_near_body(
    windows, own, left, right, own_in, left_in, right_in, queries, before, after,
    sums, stats, keys, values, peak, total, mixed, counts, sems,
):
    def start(at):
        peak[...] = jnp.full(peak.shape, NEVER, jnp.float32)
        total[...] = jnp.zeros(total.shape, jnp.float32)
        mixed[...] = jnp.zeros(mixed.shape, jnp.float32)

    def finish(at):
        sums[at] = mixed[...]
        row = lax.broadcasted_iota(jnp.int32, stats.shape[1:], 0)
        stats[at] = jnp.where(row == 0, peak[...], total[...])

    tables = {
        (0, 0): own, (0, 2): own_in, (1, 0): left, (1, 2): left_in, (2, 0): right, (2, 2): right_in
    }
    asked = (queries, before, after)
    wide_walk(
        windows, tables, asked, start, keys, values, peak, total, mixed, counts, sems, finish
    )


def wide_far_body(
    windows, own, left, right, queries, before, after, held_sums, held_stats,
    sums, stats, out0, out1, keys, values, peak, total, mixed, counts, sems,
):
    tokens = queries.shape[2]

    def start(at):
        peak[...] = held_stats[at, 0:1]
        total[...] = held_stats[at, 1:2]
        mixed[...] = held_sums[at]

    def finish(at):
        sums[at] = mixed[:, :tokens]
        row = lax.broadcasted_iota(jnp.int32, stats.shape[1:], 0)
        stats[at] = jnp.where(row == 0, peak[:, :tokens], total[:, :tokens])
        for part, out in ((1, out0), (2, out1)):
            some = slice(part * tokens, (part + 1) * tokens)
            top = high(low(peak[:, some]))
            factor = jnp.exp2(peak[:, some] - top)
            whole = total[:, some] * factor
            big = high(low(whole))
            row = lax.broadcasted_iota(jnp.int32, (16, tokens), 0)
            held = jnp.where(row == 0, top, jnp.where(row == 1, big, whole - big))
            out[at, :DEPTH] = low(mixed[:, some] * factor)
            out[at, DEPTH:] = low(held)

    tables = {(0, 1): own, (1, 1): left, (2, 1): right}
    asked = (queries, before, after)
    wide_walk(
        windows, tables, asked, start, keys, values, peak, total, mixed, counts, sems, finish
    )


def text_merge_body(query, count, got, got_other, after, out):
    heads = query.shape[1] // DEPTH
    core = lax.axis_index("co")
    chip = (
        lax.axis_index("ta") * lax.axis_size("ha") + lax.axis_index("ha")
    ) * lax.axis_size("zh") + lax.axis_index("zh")
    sources = got.shape[0] // SLOTS
    at = core * sources + chip
    block = high(query[pl.ds(pl.multiple_of(at // 16 * 16, 16), 16), :])
    row = lax.broadcasted_iota(jnp.int32, block.shape, 0)
    asked = jnp.sum(jnp.where(row == at % 16, block, 0.0), axis=0, keepdims=True)
    near, far = text_masks(count[0], sources, 1)
    stats = got[slot(heads)]
    blocks = []
    for head in range(heads):
        peak = stats[:, head : head + 1]
        mine = asked[:, head * DEPTH : (head + 1) * DEPTH]
        key_at, value_at = slot(heads + 1 + head), slot(2 * heads + 1 + head)
        first = jnp.sum(got[key_at] * mine, axis=1, keepdims=True) * SCALE
        second = jnp.sum(got_other[key_at] * mine, axis=1, keepdims=True) * SCALE
        first = jnp.where(near, first, NEVER)
        second = jnp.where(far, second, NEVER)
        top = jnp.max(jnp.maximum(peak, jnp.maximum(first, second)), axis=0, keepdims=True)
        factor = jnp.exp2(peak - top)
        first = jnp.exp2(first - top)
        second = jnp.exp2(second - top)
        whole = jnp.sum(
            factor * stats[:, 16 + head : 17 + head] + first + second, axis=0, keepdims=True
        )
        mixed = jnp.sum(
            factor * got[slot(head)] + first * got[value_at] + second * got_other[value_at],
            axis=0,
            keepdims=True,
        )
        blocks.append(mixed / whole)
    blocks.append(jnp.zeros((ENDS - heads, DEPTH), jnp.float32))
    chunk = jnp.concatenate(blocks, axis=0)
    for source in range(sources):
        out[source * ENDS : (source + 1) * ENDS] = chunk


def text_out_body(mine, other, out):
    half = mine.shape[0] // ENDS
    heads = out.shape[1] // DEPTH
    core = lax.axis_index("co")
    for source, place in ((mine, core), (other, 1 - core)):
        rows = pl.ds(pl.multiple_of(place * half, half), half)
        for head in range(heads):
            picked = source[pl.ds(head, half, stride=ENDS), :]
            out[rows, head * DEPTH : (head + 1) * DEPTH] = low(picked)


def final_body(
    windows, sums, stats, text_sums, text_stats, back0, back1, narrow, w_own, w_mine, w_other,
    hidden, modulation, final, out, attended, weight, updated, residual,
    spread, sems, *, parts,
):
    ids = wide_heads(windows)
    branch, core = lax.axis_index("cfg"), lax.axis_index("co")
    half, model = w_own.shape
    part_cols = model // parts
    first = pltpu.make_async_copy(narrow, attended, sems.at[parts, 0])
    first.start()
    copies = []
    for part in range(parts):
        cols = pl.ds(part * part_cols, part_cols)
        for at, (source, row) in enumerate(
            (
                (w_own, branch * half),
                (w_mine, (1 - branch) * half + core * (half // 2)),
                (w_other, (1 - branch) * half + (1 - core) * (half // 2)),
            )
        ):
            rows = pl.ds(pl.multiple_of(row, half // 2), source.shape[0])
            copies.append(
                pltpu.make_async_copy(
                    source.at[:, cols], weight.at[rows, cols], sems.at[part, at]
                )
            )
        copies.append(
            pltpu.make_async_copy(hidden.at[:, cols], residual.at[:, cols], sems.at[part, 3])
        )
    for copy in copies:
        copy.start()
    time_at = lax.axis_index("ta")
    inside = (time_at > 0, time_at < lax.axis_size("ta") - 1)
    first.wait()
    for at in range(WIDE):
        peaks = [stats[at, 0:1], text_stats[at, 0:1]]
        totals = [stats[at, 1:2], text_stats[at, 1:2]]
        for back, ok in zip((back0, back1), inside):
            rows = high(back[at, DEPTH:])
            peaks.append(jnp.where(ok, rows[0:1], NEVER))
            totals.append(jnp.where(ok, rows[1:2] + rows[2:3], 0.0))
        top = functools.reduce(jnp.maximum, peaks)
        factors = [jnp.exp2(peak - top) for peak in peaks]
        total = sum(factor * whole for factor, whole in zip(factors, totals))
        mixed = (
            sums[at] * factors[0]
            + text_sums[at] * factors[1]
            + high(back0[at, :DEPTH]) * factors[2]
            + high(back1[at, :DEPTH]) * factors[3]
        )
        attended[:, lanes(ids[at])] = low((mixed / total).T)
    tokens = attended.shape[0]
    pivot = None
    running = jnp.zeros((tokens, DEPTH), jnp.float32)
    squares = jnp.zeros((tokens, DEPTH), jnp.float32)
    for part in range(parts):
        cols = slice(part * part_cols, (part + 1) * part_cols)
        for copy in copies[4 * part : 4 * part + 4]:
            copy.wait()
        projected = inner(attended[...], weight[:, cols])
        fresh = high(residual[:, cols]) + modulation[0, :, cols] * projected
        if pivot is None:
            pivot = jnp.sum(fresh, axis=1, keepdims=True) / part_cols
        fresh = fresh - pivot
        updated[:, cols] = fresh
        for lane in range(0, part_cols, DEPTH):
            some = fresh[:, lane : lane + DEPTH]
            running = running + some
            squares = squares + some * some
    mean = jnp.sum(running, axis=1, keepdims=True) / model
    variance = jnp.sum(squares, axis=1, keepdims=True) / model - mean * mean
    factor = lax.rsqrt(jnp.maximum(variance, 0.0) + 1e-06)
    channels = final.shape[0]
    result = jnp.zeros((tokens, channels), jnp.float32)
    for part in range(parts):
        cols = slice(part * part_cols, (part + 1) * part_cols)
        normed = (updated[:, cols] - mean) * factor * (1.0 + modulation[2, :, cols])
        normed = normed + modulation[1, :, cols]
        result = result + outer(low(normed), final[:, cols])
    spread[:, :channels] = result
    columns = out.shape[1] // channels
    for column in range(columns):
        out[:, column * channels : (column + 1) * channels] = spread[
            pl.ds(column, tokens // columns, stride=columns), :
        ][:, :channels]


def shift(x, axis, step):
    size = lax.axis_size(axis)
    return lax.ppermute(x, axis, [(i, i + step) for i in range(size) if 0 <= i + step < size])


def swap_core(x):
    return lax.ppermute(x, "co", [(0, 1), (1, 0)])


def local(
    video_query, video_key, video_value, text_query, text_key, text_value, text_count, head_windows,
    hidden_state, out_weight, final_weight, modulation, guidance,
):
    frames, rows, cols, width = video_query.shape[1:]
    tokens = frames * rows * cols
    heads = head_windows.shape[0]
    text_len = text_query.shape[1]
    half_text = text_len // 2
    model = out_weight.shape[1]
    half_width = out_weight.shape[0]
    bf16, f32 = jnp.bfloat16, jnp.float32
    shape = jax.ShapeDtypeStruct
    query = video_query.reshape(tokens, width)
    key = video_key.reshape(tokens, width)
    value = video_value.reshape(tokens, width)
    text_query = text_query[0]
    windows = head_windows.T
    core = lax.axis_index("co")
    branch = lax.axis_index("cfg")
    zones = lax.axis_size("zh")

    pairs, queries = call(
        pack_body,
        (shape((2 * WIDE, tokens, DEPTH), bf16), shape((WIDE, DEPTH, tokens), bf16)),
        [SMEM, HBM, HBM, HBM],
        (VMEM, VMEM),
        [pltpu.VMEM((2 * WIDE, tokens, DEPTH), bf16), pltpu.SemaphoreType.DMA((3 * WIDE,))],
        8, 0, 4 * MIB,
        windows, query, key, value,
    )
    beside = [(2 * z + 1, 2 * z + 2) for z in range(zones - 1)]
    beside = beside + [(b, a) for a, b in beside]
    next_pairs = lax.ppermute(pairs, ("zh", "co"), beside)
    from_before = shift(queries, "ta", 1)
    from_after = shift(queries, "ta", -1)
    pairs_in = swap_core(pairs)
    left = shift(pairs, "ha", 1)
    right = shift(pairs, "ha", -1)

    part_shape = shape((half_text, width), f32)
    stat_shape = shape((half_text, DEPTH), f32)
    text_sums, far_sums, text_stats, far_stats = call(
        text_video_body,
        (part_shape, part_shape, stat_shape, stat_shape),
        [VMEM] * 3 + [HBM], (VMEM,) * 4, [pltpu.VMEM((DEPTH, DEPTH), f32)],
        16, 4 * text_len * tokens * width, 4 * tokens * width,
        text_query, key, value, pairs,
    )
    parcel = call(
        text_join_body,
        shape((SLOTS * half_text, DEPTH), f32),
        [VMEM] * 6 + [HBM] * 3, VMEM, [], 12, 0, 2 * MIB,
        text_sums, text_stats, swap_core(far_sums), swap_core(far_stats), text_key[0], text_value[0],
        next_pairs, left, right,
    )

    next_left = shift(next_pairs, "ha", 1)
    next_right = shift(next_pairs, "ha", -1)
    left_in = swap_core(left)
    right_in = swap_core(right)

    def at(branch_at, zone, core_at):
        return (branch_at * zones + zone) * 2 + core_at

    weight_pairs = []
    for z in range(zones):
        weight_pairs.append((at(0, z, 0), at(1, z, 0)))
        weight_pairs.append((at(0, (z + 1) % zones, 1), at(1, z, 1)))
    weight_pairs = weight_pairs + [(b, a) for a, b in weight_pairs]
    quarter = call(
        quarter_body,
        shape((half_width // 2, model), bf16),
        [HBM] * 2, HBM,
        [pltpu.VMEM((half_width // 2, model), bf16), pltpu.SemaphoreType.DMA((2, 4))],
        8, 0, 2 * half_width * model,
        out_weight, next_pairs,
    )
    w_mine = lax.ppermute(quarter, ("cfg", "zh", "co"), weight_pairs)
    parcel = after(parcel, quarter, pairs_in, left_in, right_in, from_before, from_after)
    got = lax.all_to_all(parcel, CHIPS, 0, 0, tiled=True)
    wide_sums = shape((WIDE, DEPTH, tokens), f32)
    wide_stats = shape((WIDE, 8, tokens), f32)
    lent = shape((WIDE, DEPTH + 16, tokens), bf16)
    def wide_scratch(places):
        return [
            pltpu.VMEM((WIDE, places * tokens, DEPTH), bf16),
            pltpu.VMEM((WIDE, places * tokens, DEPTH), bf16),
            pltpu.VMEM((1, 3 * tokens), f32),
            pltpu.VMEM((1, 3 * tokens), f32),
            pltpu.VMEM((DEPTH, 3 * tokens), f32),
            pltpu.SMEM((2 * WIDE,), jnp.int32),
            pltpu.SemaphoreType.DMA((WIDE * places, 2)),
        ]

    near_sums, near_stats = call(
        wide_near_body,
        (shape((WIDE, DEPTH, 3 * tokens), f32), shape((WIDE, 8, 3 * tokens), f32)),
        [SMEM] + [HBM] * 6 + [VMEM] * 3, (VMEM,) * 2,
        wide_scratch(6),
        24, 12 * WIDE * 6 * tokens * tokens * DEPTH, 8 * MIB,
        windows, pairs, left, right, pairs_in, left_in, right_in, queries, from_before, from_after,
    )
    sums, stats, to_before, to_after = call(
        wide_far_body,
        (wide_sums, wide_stats, lent, lent),
        [SMEM] + [HBM] * 3 + [VMEM] * 5, (VMEM,) * 4,
        wide_scratch(3),
        24, 12 * WIDE * 3 * tokens * tokens * DEPTH, 8 * MIB,
        windows, next_pairs, next_left, next_right, queries, from_before, from_after,
        near_sums, near_stats,
    )
    back_after = shift(to_before, "ta", -1)
    back_before = shift(to_after, "ta", 1)

    got = after(got, to_before)
    got_other = swap_core(got)
    finished = call(
        text_merge_body,
        shape((ENDS * half_text, DEPTH), f32),
        [VMEM, SMEM, VMEM, VMEM, HBM], VMEM, [], 16, 0, 3 * MIB,
        text_query, text_count, got, got_other, to_before,
    )
    finished = after(finished, back_before, back_after)
    w_mine = after(w_mine, finished)
    w_other = swap_core(w_mine)
    narrow, beside_sums, beside_stats = call(
        narrow_body,
        (shape((tokens, width), bf16), wide_sums, wide_stats),
        [SMEM, SMEM] + [VMEM] * 6 + [HBM], (VMEM,) * 3,
        [
            pltpu.VMEM((heads, text_len, DEPTH), bf16),
            pltpu.VMEM((heads, text_len, DEPTH), bf16),
            pltpu.SMEM((heads + 1,), jnp.int32),
        ],
        24, 4 * (heads - WIDE) * tokens * (tokens + text_len) * DEPTH, 5 * tokens * width * 2,
        windows, text_count, query, key, value, queries, got, got_other, finished,
    )

    text_mine = lax.all_to_all(finished, CHIPS, 0, 0, tiled=True)
    parts = 6
    branch_out = call(
        functools.partial(final_body, parts=parts),
        shape((frames * rows, cols * final_weight.shape[1]), f32),
        [SMEM] + [VMEM] * 6 + [HBM] * 5 + [VMEM] * 2, VMEM,
        [
            pltpu.VMEM((tokens, width), bf16),
            pltpu.VMEM((width, model), bf16),
            pltpu.VMEM((tokens, model), f32),
            pltpu.VMEM((tokens, model), bf16),
            pltpu.VMEM((tokens, DEPTH), f32),
            pltpu.SemaphoreType.DMA((parts + 1, 4)),
        ],
        40, 2 * tokens * width * model, 16 * MIB,
        windows, sums, stats, beside_sums, beside_stats, back_before, back_after, narrow,
        out_weight, w_mine, w_other,
        hidden_state.reshape(tokens, model), modulation.transpose(1, 0, 2), final_weight.T,
    )
    text_mine = after(text_mine, branch_out)
    text_out = call(
        text_out_body, shape((text_len, width), bf16), [VMEM, VMEM], VMEM, [], 8, 0, MIB,
        text_mine, swap_core(text_mine),
    )
    half_rows = rows // 2
    grid = branch_out.reshape(frames, rows, cols * final_weight.shape[1])
    kept = lax.dynamic_slice_in_dim(grid, branch * half_rows, half_rows, 1)
    sent = lax.dynamic_slice_in_dim(grid, (1 - branch) * half_rows, half_rows, 1)
    received = lax.ppermute(sent, "cfg", [(0, 1), (1, 0)])
    conditional = jnp.where(branch == 0, kept, received)
    unconditional = jnp.where(branch == 0, received, kept)
    guided = unconditional + guidance[0] * (conditional - unconditional)
    return (guided, text_out[None])


def solution(mesh):
    devices = mesh.devices.reshape(mesh.devices.shape[:3] + (mesh.devices.shape[3] // 2, 2))
    split = Mesh(devices, ("cfg", "ta", "ha", "zh", "co"))
    wa = ("zh", "co")
    everyone = ("ta", "ha", "zh", "co")
    video = P("cfg", "ta", "ha", wa, None)
    in_specs = (
        video, video, video,
        P("cfg", None, None),
        P("cfg", everyone, None),
        P("cfg", everyone, None),
        P("cfg"),
        P(),
        video,
        P("cfg", None),
        P(),
        P("cfg", None, None),
        P(),
    )
    out_specs = (P("ta", ("ha", "cfg"), wa), P("cfg", None, None))
    return jax.shard_map(local, mesh=split, in_specs=in_specs, out_specs=out_specs, check_vma=False)
```

```python
import functools
import math

import jax
import jax.numpy as jnp
from jax import lax
from jax.experimental import pallas as pl
from jax.experimental.pallas import tpu as pltpu
from jax.sharding import Mesh
from jax.sharding import PartitionSpec as P

DEPTH = 128
WIDE = 3
NEVER = -(2.0**100)
CHIPS = ("ta", "ha", "zh")
SLOTS = 56
ENDS = 16
LOG2E = math.log2(math.e)
SCALE = LOG2E / math.sqrt(DEPTH)
MIB = 1024 * 1024

VMEM = pl.BlockSpec(memory_space=pltpu.VMEM)
SMEM = pl.BlockSpec(memory_space=pltpu.SMEM)
HBM = pl.BlockSpec(memory_space=pl.ANY)


def call(body, out_shape, in_specs, out_specs, scratch, vmem, flops, moved, *operands):
    return pl.pallas_call(
        body,
        grid=(1,),
        out_shape=out_shape,
        in_specs=in_specs,
        out_specs=out_specs,
        scratch_shapes=scratch,
        compiler_params=pltpu.CompilerParams(vmem_limit_bytes=64 * MIB - 65536),
        cost_estimate=pl.CostEstimate(flops=flops, bytes_accessed=moved, transcendentals=0),
    )(*operands)


def lanes(head):
    return pl.ds(pl.multiple_of(head * DEPTH, DEPTH), DEPTH)


def wide_heads(windows):
    found = jnp.int32(0)
    ids = [jnp.int32(0)] * WIDE
    for head in range(windows.shape[1]):
        wide = (windows[0, head] > 1) | (windows[1, head] > 1) | (windows[2, head] > 1)
        for at in range(WIDE):
            ids[at] = jnp.where(wide & (found == at), head, ids[at])
        found = found + wide.astype(jnp.int32)
    return ids


def outer(a, b):
    return lax.dot_general(a, b, (((1,), (1,)), ((), ())), preferred_element_type=jnp.float32)


def inner(a, b):
    return jnp.dot(a, b, preferred_element_type=jnp.float32)


def low(x):
    return x.astype(jnp.bfloat16)


def high(x):
    return x.astype(jnp.float32)


def slot(index):
    return pl.ds(index, 64, stride=SLOTS), slice(None)


def after_body(*refs):
    pass


def after(x, *others):
    return pl.pallas_call(
        after_body,
        out_shape=jax.ShapeDtypeStruct(x.shape, x.dtype),
        in_specs=[HBM] * (1 + len(others)),
        out_specs=HBM,
        input_output_aliases={0: 0},
    )(x, *others)


def front_body(
    windows, text, query, key_at, value_at, weight,
    pairs, queries, quarter, own_sums, far_sums, own_stats, far_stats,
    key, value, held, stats, passing, sems, weight_sems,
):
    ids = wide_heads(windows)
    tokens = query.shape[0]
    copies = [
        pltpu.make_async_copy(key_at, key, sems.at[WIDE]),
        pltpu.make_async_copy(value_at, value, sems.at[WIDE + 1]),
    ]
    for at in range(WIDE):
        copies.append(pltpu.make_async_copy(query.at[:, lanes(ids[at])], held.at[at], sems.at[at]))
    for copy in copies:
        copy.start()
    core = lax.axis_index("co")
    rows = quarter.shape[0]
    chunk = rows // 4
    loads = []
    stores = []
    for at in range(4):
        source = pl.ds(pl.multiple_of(core * rows + at * chunk, chunk), chunk)
        here = pl.ds(at * chunk, chunk)
        loads.append(
            pltpu.make_async_copy(weight.at[source, :], passing.at[here], weight_sems.at[0, at])
        )
        stores.append(
            pltpu.make_async_copy(passing.at[here], quarter.at[here], weight_sems.at[1, at])
        )
    for copy in copies:
        copy.wait()
    for load in loads:
        load.start()
    for at in range(WIDE):
        queries[at] = held[at].T
        pairs[at] = key[:, lanes(ids[at])]
        picked = value[:, lanes(ids[at])]
        for row in range(0, tokens, DEPTH):
            pairs[WIDE + at, row : row + DEPTH] = picked[row : row + DEPTH].T
    half = own_sums.shape[0]
    own_rows = pl.ds(pl.multiple_of(core * half, half), half)
    far_rows = pl.ds(pl.multiple_of((1 - core) * half, half), half)
    stats[...] = jnp.zeros(stats.shape, jnp.float32)
    for head in range(text.shape[1] // DEPTH):
        if head % 3 == 2:
            loads[head // 3].wait()
            stores[head // 3].start()
        cols = slice(head * DEPTH, (head + 1) * DEPTH)
        asked = jnp.concatenate((text[own_rows, cols], text[far_rows, cols]), axis=0).T
        scores = inner(key[:, cols], asked) * SCALE
        peak = jnp.max(scores, axis=0, keepdims=True)
        weights = jnp.exp2(scores - peak)
        stats[head : head + 1] = peak
        stats[16 + head : 17 + head] = jnp.sum(weights, axis=0, keepdims=True)
        mixed = inner(low(weights).T, value[:, cols])
        own_sums[:, cols] = mixed[:half]
        far_sums[:, cols] = mixed[half:]
    turned = stats[...].T
    own_stats[...] = turned[:half]
    far_stats[...] = turned[half:]
    for store in stores:
        store.wait()


def text_join_body(sums, stats, far_sums, far_stats, text_key, text_value, *rest):
    parcel, out = rest[-2:]
    half, width = sums.shape
    heads = width // DEPTH
    lane = lax.broadcasted_iota(jnp.int32, stats.shape, 1)
    held = jnp.zeros(stats.shape, jnp.float32)
    for head in range(heads):
        cols = slice(head * DEPTH, (head + 1) * DEPTH)
        first, second = stats[:, head : head + 1], far_stats[:, head : head + 1]
        top = high(low(jnp.maximum(first, second)))
        first, second = jnp.exp2(first - top), jnp.exp2(second - top)
        total = stats[:, 16 + head : 17 + head] * first + far_stats[:, 16 + head : 17 + head] * second
        mixed = sums[:, cols] * first + far_sums[:, cols] * second
        coarse = high(low(mixed))
        out[slot(head)] = coarse
        out[slot(heads + head)] = mixed - coarse
        big = high(low(total))
        held = jnp.where(lane == head, top, held)
        held = jnp.where(lane == 16 + head, big, held)
        held = jnp.where(lane == 32 + head, total - big, held)
        out[slot(2 * heads + 1 + head)] = jnp.broadcast_to(high(text_key[:, cols]), (half, DEPTH))
        out[slot(3 * heads + 1 + head)] = jnp.broadcast_to(high(text_value[:, cols]), (half, DEPTH))
    out[slot(2 * heads)] = held
    spare = jnp.zeros((half, DEPTH), jnp.float32)
    for index in range(4 * heads + 1, SLOTS):
        out[slot(index)] = spare
    parcel[...] = low(out[...])


def text_masks(count, rows, cols):
    place = 2 * lax.broadcasted_iota(jnp.int32, (rows, cols), 0)
    core = lax.axis_index("co")
    return place + core < count, place + 1 - core < count


def back_body(
    windows, count, text, query, key, value, queries, got_low, got_other_low, after,
    finished, out, sums, stats, text_keys, text_values, ids, got, got_other,
):
    got[...] = high(got_low[...])
    got_other[...] = high(got_other_low[...])
    text_merge(text, count, got, got_other, finished)
    heads = windows.shape[1]
    half = got.shape[0] // SLOTS
    for head in range(heads):
        for at, source in enumerate((got, got_other)):
            rows = slice(at * half, (at + 1) * half)
            text_keys[head, rows] = low(source[slot(2 * heads + 1 + head)])
            text_values[head, rows] = low(source[slot(3 * heads + 1 + head)])
    found = jnp.int32(0)
    for head in range(heads):
        wide = (windows[0, head] > 1) | (windows[1, head] > 1) | (windows[2, head] > 1)
        ids[jnp.where(wide, heads, found)] = head
        found = found + 1 - wide.astype(jnp.int32)
    tokens = query.shape[0]
    valid = jnp.concatenate(
        [high(mask.astype(jnp.int32)) for mask in text_masks(count[0], half, DEPTH)], axis=0
    ) > 0.5

    def step(group, carry):
        for at in range(3):
            head = ids[group * 3 + at]
            cols = lanes(head)
            keys = jnp.concatenate((key[:, cols], text_keys[head]), axis=0)
            values = jnp.concatenate((value[:, cols], text_values[head]), axis=0).T
            asked = query[:, cols].T
            for first in range(0, tokens, DEPTH):
                scores = inner(keys, asked[:, first : first + DEPTH]) * SCALE
                near, text = scores[:tokens], jnp.where(valid, scores[tokens:], NEVER)
                peak = jnp.maximum(
                    jnp.max(near, axis=0, keepdims=True), jnp.max(text, axis=0, keepdims=True)
                )
                weights = jnp.exp2(jnp.concatenate((near, text), axis=0) - peak)
                total = jnp.sum(weights, axis=0, keepdims=True)
                mixed = inner(values, low(weights))
                out[first : first + DEPTH, cols] = low((mixed / total).T)
        return carry

    lax.fori_loop(0, (heads - WIDE) // 3, step, 0)
    row = lax.broadcasted_iota(jnp.int32, (stats.shape[1], DEPTH), 0)
    for at, head in enumerate(wide_heads(windows)):
        keys = text_keys[head]
        values = text_values[head].T
        for first in range(0, tokens, DEPTH):
            some = slice(first, first + DEPTH)
            scores = jnp.where(valid, inner(keys, queries[at, :, some]) * SCALE, NEVER)
            peak = jnp.max(scores, axis=0, keepdims=True)
            weights = jnp.exp2(scores - peak)
            stats[at, :, some] = jnp.where(row == 0, peak, jnp.sum(weights, axis=0, keepdims=True))
            sums[at, :, some] = inner(values, low(weights))


def place_ok(windows, head, a, c):
    row_at, zone, core = lax.axis_index("ha"), lax.axis_index("zh"), lax.axis_index("co")
    ok = jnp.bool_(True)
    if a > 0:
        ok = windows[1, head] > 1
        ok = ok & ((row_at > 0) if a == 1 else (row_at < lax.axis_size("ha") - 1))
    if c > 0:
        ok = ok & (windows[2, head] > 1)
    if c == 1:
        ok = ok & jnp.where(core == 0, zone > 0, zone < lax.axis_size("zh") - 1)
    return ok


def wide_walk(
    windows, tables, asked, before, keys, values, peak, total, mixed, counts, sems, finish
):
    ids = wide_heads(windows)
    tokens = asked[0].shape[2]
    places = list(tables)
    for at in range(WIDE):
        found = jnp.int32(0)
        for number, (a, c) in enumerate(places):
            source = tables[a, c]
            ok = place_ok(windows, ids[at], a, c)
            slot_at = at * len(places) + number
            rows = pl.ds(pl.multiple_of(found * tokens, tokens), tokens)

            @pl.when(ok)
            def _(source=source, slot_at=slot_at, rows=rows, at=at):
                pltpu.make_async_copy(source.at[at], keys.at[at, rows], sems.at[slot_at, 0]).start()
                pltpu.make_async_copy(
                    source.at[WIDE + at], values.at[at, rows], sems.at[slot_at, 1]
                ).start()

            found = found + ok.astype(jnp.int32)
        counts[at] = found
        counts[WIDE + at] = ids[at]
    any_tile = tables[places[0]]

    def head_step(at, carry):
        head = counts[WIDE + at]
        count = counts[at]
        for number, (a, c) in enumerate(places):

            @pl.when(place_ok(windows, head, a, c))
            def _(number=number):
                slot_at = at * len(places) + number
                whole = pl.ds(0, tokens)
                pltpu.make_async_copy(any_tile.at[0], keys.at[at, whole], sems.at[slot_at, 0]).wait()
                pltpu.make_async_copy(any_tile.at[0], values.at[at, whole], sems.at[slot_at, 1]).wait()

        before(at)

        def span(start, size, sources):
            rows = pl.ds(pl.multiple_of(start, tokens), size)
            key = keys[at, rows]
            value = values[at, rows]
            value = jnp.concatenate(
                [value[row : row + DEPTH] for row in range(0, size, DEPTH)], axis=1
            )
            for part, source in sources:
                for first in range(0, tokens, DEPTH):
                    some = slice(part * tokens + first, part * tokens + first + DEPTH)
                    scores = inner(key, source[at, :, first : first + DEPTH]) * SCALE
                    held = peak[:, some]
                    top = jnp.maximum(held, jnp.max(scores, axis=0, keepdims=True))
                    factor = jnp.exp2(held - top)
                    weights = jnp.exp2(scores - top)
                    total[:, some] = total[:, some] * factor + jnp.sum(
                        weights, axis=0, keepdims=True
                    )
                    mixed[:, some] = mixed[:, some] * factor + inner(value, low(weights))
                    peak[:, some] = top

        def spans(sources):
            @pl.when(count == len(places))
            def _():
                span(0, len(places) * tokens, sources)

            @pl.when(count < len(places))
            def _():
                threes = count // 3 if len(places) > 3 else 0

                def three(step, carry):
                    span(step * 3 * tokens, 3 * tokens, sources)
                    return carry

                def one(step, carry):
                    span(step * tokens, tokens, sources)
                    return carry

                if len(places) > 3:
                    lax.fori_loop(0, threes, three, 0)
                lax.fori_loop(threes * 3, count, one, 0)

        spans(((0, asked[0]),))

        @pl.when(windows[0, head] > 1)
        def _():
            spans(((1, asked[1]), (2, asked[2])))

        finish(at)
        return carry

    lax.fori_loop(0, WIDE, head_step, 0)


def wide_near_body(
    windows, own, left, right, own_in, left_in, right_in, queries, before, after,
    sums, stats, keys, values, peak, total, mixed, counts, sems,
):
    def start(at):
        peak[...] = jnp.full(peak.shape, NEVER, jnp.float32)
        total[...] = jnp.zeros(total.shape, jnp.float32)
        mixed[...] = jnp.zeros(mixed.shape, jnp.float32)

    def finish(at):
        sums[at] = mixed[...]
        row = lax.broadcasted_iota(jnp.int32, stats.shape[1:], 0)
        stats[at] = jnp.where(row == 0, peak[...], total[...])

    tables = {
        (0, 0): own, (0, 2): own_in, (1, 0): left, (1, 2): left_in, (2, 0): right, (2, 2): right_in
    }
    asked = (queries, before, after)
    wide_walk(
        windows, tables, asked, start, keys, values, peak, total, mixed, counts, sems, finish
    )


def wide_far_body(
    windows, own, left, right, queries, before, after, held_sums, held_stats,
    sums, stats, out0, out1, keys, values, peak, total, mixed, counts, sems,
):
    tokens = queries.shape[2]

    def start(at):
        peak[...] = held_stats[at, 0:1]
        total[...] = held_stats[at, 1:2]
        mixed[...] = held_sums[at]

    def finish(at):
        sums[at] = mixed[:, :tokens]
        row = lax.broadcasted_iota(jnp.int32, stats.shape[1:], 0)
        stats[at] = jnp.where(row == 0, peak[:, :tokens], total[:, :tokens])
        for part, out in ((1, out0), (2, out1)):
            some = slice(part * tokens, (part + 1) * tokens)
            top = high(low(peak[:, some]))
            factor = jnp.exp2(peak[:, some] - top)
            whole = total[:, some] * factor
            big = high(low(whole))
            row = lax.broadcasted_iota(jnp.int32, (16, tokens), 0)
            held = jnp.where(row == 0, top, jnp.where(row == 1, big, whole - big))
            out[at, :DEPTH] = low(mixed[:, some] * factor)
            out[at, DEPTH:] = low(held)

    tables = {(0, 1): own, (1, 1): left, (2, 1): right}
    asked = (queries, before, after)
    wide_walk(
        windows, tables, asked, start, keys, values, peak, total, mixed, counts, sems, finish
    )


def text_merge(query, count, got, got_other, out):
    heads = query.shape[1] // DEPTH
    core = lax.axis_index("co")
    chip = (
        lax.axis_index("ta") * lax.axis_size("ha") + lax.axis_index("ha")
    ) * lax.axis_size("zh") + lax.axis_index("zh")
    sources = got.shape[0] // SLOTS
    at = core * sources + chip
    block = high(query[pl.ds(pl.multiple_of(at // 16 * 16, 16), 16), :])
    row = lax.broadcasted_iota(jnp.int32, block.shape, 0)
    asked = jnp.sum(jnp.where(row == at % 16, block, 0.0), axis=0, keepdims=True)
    near, far = text_masks(count[0], sources, 1)
    stats = got[slot(2 * heads)]
    blocks = []
    for head in range(heads):
        peak = stats[:, head : head + 1]
        mine = asked[:, head * DEPTH : (head + 1) * DEPTH]
        key_at, value_at = slot(2 * heads + 1 + head), slot(3 * heads + 1 + head)
        first = jnp.sum(got[key_at] * mine, axis=1, keepdims=True) * SCALE
        second = jnp.sum(got_other[key_at] * mine, axis=1, keepdims=True) * SCALE
        first = jnp.where(near, first, NEVER)
        second = jnp.where(far, second, NEVER)
        top = jnp.max(jnp.maximum(peak, jnp.maximum(first, second)), axis=0, keepdims=True)
        factor = jnp.exp2(peak - top)
        first = jnp.exp2(first - top)
        second = jnp.exp2(second - top)
        whole = jnp.sum(
            factor * (stats[:, 16 + head : 17 + head] + stats[:, 32 + head : 33 + head])
            + first
            + second,
            axis=0,
            keepdims=True,
        )
        mixed = jnp.sum(
            factor * (got[slot(head)] + got[slot(heads + head)]) + first * got[value_at] + second * got_other[value_at],
            axis=0,
            keepdims=True,
        )
        blocks.append(mixed / whole)
    blocks.append(jnp.zeros((ENDS - heads, DEPTH), jnp.float32))
    chunk = jnp.concatenate(blocks, axis=0)
    for source in range(sources):
        out[source * ENDS : (source + 1) * ENDS] = chunk


def text_out_body(mine, other, out):
    half = mine.shape[0] // ENDS
    heads = out.shape[1] // DEPTH
    core = lax.axis_index("co")
    for source, place in ((mine, core), (other, 1 - core)):
        rows = pl.ds(pl.multiple_of(place * half, half), half)
        for head in range(heads):
            picked = source[pl.ds(head, half, stride=ENDS), :]
            out[rows, head * DEPTH : (head + 1) * DEPTH] = low(picked)


def final_body(
    windows, sums, stats, text_sums, text_stats, back0, back1, narrow, w_own, w_mine, w_other,
    hidden, modulation, final, out, attended, weight, updated, residual,
    spread, sems, *, parts,
):
    ids = wide_heads(windows)
    branch, core = lax.axis_index("cfg"), lax.axis_index("co")
    half, model = w_own.shape
    part_cols = model // parts
    first = pltpu.make_async_copy(narrow, attended, sems.at[parts, 0])
    first.start()
    copies = []
    for part in range(parts):
        cols = pl.ds(part * part_cols, part_cols)
        for at, (source, row) in enumerate(
            (
                (w_own, branch * half),
                (w_mine, (1 - branch) * half + core * (half // 2)),
                (w_other, (1 - branch) * half + (1 - core) * (half // 2)),
            )
        ):
            rows = pl.ds(pl.multiple_of(row, half // 2), source.shape[0])
            copies.append(
                pltpu.make_async_copy(
                    source.at[:, cols], weight.at[rows, cols], sems.at[part, at]
                )
            )
        copies.append(
            pltpu.make_async_copy(hidden.at[:, cols], residual.at[:, cols], sems.at[part, 3])
        )
    for copy in copies:
        copy.start()
    time_at = lax.axis_index("ta")
    inside = (time_at > 0, time_at < lax.axis_size("ta") - 1)
    first.wait()
    for at in range(WIDE):
        peaks = [stats[at, 0:1], text_stats[at, 0:1]]
        totals = [stats[at, 1:2], text_stats[at, 1:2]]
        for back, ok in zip((back0, back1), inside):
            rows = high(back[at, DEPTH:])
            peaks.append(jnp.where(ok, rows[0:1], NEVER))
            totals.append(jnp.where(ok, rows[1:2] + rows[2:3], 0.0))
        top = functools.reduce(jnp.maximum, peaks)
        factors = [jnp.exp2(peak - top) for peak in peaks]
        total = sum(factor * whole for factor, whole in zip(factors, totals))
        mixed = (
            sums[at] * factors[0]
            + text_sums[at] * factors[1]
            + high(back0[at, :DEPTH]) * factors[2]
            + high(back1[at, :DEPTH]) * factors[3]
        )
        attended[:, lanes(ids[at])] = low((mixed / total).T)
    tokens = attended.shape[0]
    pivot = None
    running = jnp.zeros((tokens, DEPTH), jnp.float32)
    squares = jnp.zeros((tokens, DEPTH), jnp.float32)
    for part in range(parts):
        cols = slice(part * part_cols, (part + 1) * part_cols)
        for copy in copies[4 * part : 4 * part + 4]:
            copy.wait()
        projected = inner(attended[...], weight[:, cols])
        fresh = high(residual[:, cols]) + modulation[0, :, cols] * projected
        if pivot is None:
            pivot = jnp.sum(fresh, axis=1, keepdims=True) / part_cols
        fresh = fresh - pivot
        updated[:, cols] = fresh
        for lane in range(0, part_cols, DEPTH):
            some = fresh[:, lane : lane + DEPTH]
            running = running + some
            squares = squares + some * some
    mean = jnp.sum(running, axis=1, keepdims=True) / model
    variance = jnp.sum(squares, axis=1, keepdims=True) / model - mean * mean
    factor = lax.rsqrt(jnp.maximum(variance, 0.0) + 1e-06)
    channels = final.shape[0]
    result = jnp.zeros((tokens, channels), jnp.float32)
    for part in range(parts):
        cols = slice(part * part_cols, (part + 1) * part_cols)
        normed = (updated[:, cols] - mean) * factor * (1.0 + modulation[2, :, cols])
        normed = normed + modulation[1, :, cols]
        result = result + outer(low(normed), final[:, cols])
    spread[:, :channels] = result
    columns = out.shape[1] // channels
    for column in range(columns):
        out[:, column * channels : (column + 1) * channels] = spread[
            pl.ds(column, tokens // columns, stride=columns), :
        ][:, :channels]


def shift(x, axis, step):
    size = lax.axis_size(axis)
    return lax.ppermute(x, axis, [(i, i + step) for i in range(size) if 0 <= i + step < size])


def swap_core(x):
    return lax.ppermute(x, "co", [(0, 1), (1, 0)])


def local(
    video_query, video_key, video_value, text_query, text_key, text_value, text_count, head_windows,
    hidden_state, out_weight, final_weight, modulation, guidance,
):
    frames, rows, cols, width = video_query.shape[1:]
    tokens = frames * rows * cols
    heads = head_windows.shape[0]
    text_len = text_query.shape[1]
    half_text = text_len // 2
    model = out_weight.shape[1]
    half_width = out_weight.shape[0]
    bf16, f32 = jnp.bfloat16, jnp.float32
    shape = jax.ShapeDtypeStruct
    query = video_query.reshape(tokens, width)
    key = video_key.reshape(tokens, width)
    value = video_value.reshape(tokens, width)
    text_query = text_query[0]
    windows = head_windows.T
    core = lax.axis_index("co")
    branch = lax.axis_index("cfg")
    zones = lax.axis_size("zh")

    part_shape = shape((half_text, width), f32)
    stat_shape = shape((half_text, DEPTH), f32)
    pairs, queries, quarter, text_sums, far_sums, text_stats, far_stats = call(
        front_body,
        (
            shape((2 * WIDE, tokens, DEPTH), bf16), shape((WIDE, DEPTH, tokens), bf16),
            shape((half_width // 2, model), bf16), part_shape, part_shape, stat_shape, stat_shape,
        ),
        [SMEM, VMEM] + [HBM] * 4,
        (VMEM, VMEM, HBM) + (VMEM,) * 4,
        [
            pltpu.VMEM((tokens, width), bf16),
            pltpu.VMEM((tokens, width), bf16),
            pltpu.VMEM((WIDE, tokens, DEPTH), bf16),
            pltpu.VMEM((DEPTH, DEPTH), f32),
            pltpu.VMEM((half_width // 2, model), bf16),
            pltpu.SemaphoreType.DMA((WIDE + 2,)),
            pltpu.SemaphoreType.DMA((2, 4)),
        ],
        24, 0, 0,
        windows, text_query, query, key, value, out_weight,
    )
    beside = [(2 * z + 1, 2 * z + 2) for z in range(zones - 1)]
    beside = beside + [(b, a) for a, b in beside]
    next_pairs = lax.ppermute(pairs, ("zh", "co"), beside)
    pairs_in = swap_core(pairs)
    left = shift(pairs, "ha", 1)
    right = shift(pairs, "ha", -1)

    parcel = call(
        text_join_body,
        shape((SLOTS * half_text, DEPTH), bf16),
        [VMEM] * 6 + [HBM] * 2, VMEM, [pltpu.VMEM((SLOTS * half_text, DEPTH), f32)],
        16, 0, 2 * MIB,
        text_sums, text_stats, swap_core(far_sums), swap_core(far_stats), text_key[0], text_value[0],
        left, right,
    )

    next_left = shift(next_pairs, "ha", 1)
    next_right = shift(next_pairs, "ha", -1)
    left_in = swap_core(left)
    right_in = swap_core(right)

    def at(branch_at, zone, core_at):
        return (branch_at * zones + zone) * 2 + core_at

    weight_pairs = []
    for z in range(zones):
        weight_pairs.append((at(0, z, 0), at(1, z, 0)))
        weight_pairs.append((at(0, (z + 1) % zones, 1), at(1, z, 1)))
    weight_pairs = weight_pairs + [(b, a) for a, b in weight_pairs]
    queries = after(queries, parcel)
    from_before = shift(queries, "ta", 1)
    from_after = shift(queries, "ta", -1)
    parcel = after(parcel, next_pairs)
    got = lax.all_to_all(parcel, CHIPS, 0, 0, tiled=True)
    wide_sums = shape((WIDE, DEPTH, tokens), f32)
    wide_stats = shape((WIDE, 8, tokens), f32)
    lent = shape((WIDE, DEPTH + 16, tokens), bf16)
    def wide_scratch(places):
        return [
            pltpu.VMEM((WIDE, places * tokens, DEPTH), bf16),
            pltpu.VMEM((WIDE, places * tokens, DEPTH), bf16),
            pltpu.VMEM((1, 3 * tokens), f32),
            pltpu.VMEM((1, 3 * tokens), f32),
            pltpu.VMEM((DEPTH, 3 * tokens), f32),
            pltpu.SMEM((2 * WIDE,), jnp.int32),
            pltpu.SemaphoreType.DMA((WIDE * places, 2)),
        ]

    near_sums, near_stats = call(
        wide_near_body,
        (shape((WIDE, DEPTH, 3 * tokens), f32), shape((WIDE, 8, 3 * tokens), f32)),
        [SMEM] + [HBM] * 6 + [VMEM] * 3, (VMEM,) * 2,
        wide_scratch(6),
        24, 0, 0,
        windows, pairs, left, right, pairs_in, left_in, right_in, queries, from_before, from_after,
    )
    sums, stats, to_before, to_after = call(
        wide_far_body,
        (wide_sums, wide_stats, lent, lent),
        [SMEM] + [HBM] * 3 + [VMEM] * 5, (VMEM,) * 4,
        wide_scratch(3),
        24, 10**12, 0,
        windows, next_pairs, next_left, next_right, queries, from_before, from_after,
        near_sums, near_stats,
    )
    w_mine = lax.ppermute(after(quarter, near_stats), ("cfg", "zh", "co"), weight_pairs)
    back_after = shift(to_before, "ta", -1)
    back_before = shift(to_after, "ta", 1)

    got = after(got, to_before)
    got_other = swap_core(got)
    finished, narrow, beside_sums, beside_stats = call(
        back_body,
        (
            shape((ENDS * half_text, DEPTH), f32), shape((tokens, width), bf16), wide_sums,
            wide_stats,
        ),
        [SMEM, SMEM] + [VMEM] * 7 + [HBM], (VMEM,) * 4,
        [
            pltpu.VMEM((heads, text_len, DEPTH), bf16),
            pltpu.VMEM((heads, text_len, DEPTH), bf16),
            pltpu.SMEM((heads + 1,), jnp.int32),
            pltpu.VMEM((SLOTS * half_text, DEPTH), f32),
            pltpu.VMEM((SLOTS * half_text, DEPTH), f32),
        ],
        24, 4 * (heads - WIDE) * tokens * (tokens + text_len) * DEPTH, 5 * tokens * width * 2,
        windows, text_count, text_query, query, key, value, queries, got, got_other, to_before,
    )
    finished = after(finished, back_before, back_after)
    w_mine = after(w_mine, finished)
    w_other = swap_core(w_mine)
    text_mine = lax.all_to_all(finished, CHIPS, 0, 0, tiled=True)

    parts = 6
    branch_out = call(
        functools.partial(final_body, parts=parts),
        shape((frames * rows, cols * final_weight.shape[1]), f32),
        [SMEM] + [VMEM] * 6 + [HBM] * 5 + [VMEM] * 2, VMEM,
        [
            pltpu.VMEM((tokens, width), bf16),
            pltpu.VMEM((width, model), bf16),
            pltpu.VMEM((tokens, model), f32),
            pltpu.VMEM((tokens, model), bf16),
            pltpu.VMEM((tokens, DEPTH), f32),
            pltpu.SemaphoreType.DMA((parts + 1, 4)),
        ],
        40, 2 * tokens * width * model, 16 * MIB,
        windows, sums, stats, beside_sums, beside_stats, back_before, back_after, narrow,
        out_weight, w_mine, w_other,
        hidden_state.reshape(tokens, model), modulation.transpose(1, 0, 2), final_weight.T,
    )
    text_mine = after(text_mine, branch_out)
    text_out = call(
        text_out_body, shape((text_len, width), bf16), [VMEM, VMEM], VMEM, [], 8, 0, MIB,
        text_mine, swap_core(text_mine),
    )
    half_rows = rows // 2
    grid = branch_out.reshape(frames, rows, cols * final_weight.shape[1])
    kept = lax.dynamic_slice_in_dim(grid, branch * half_rows, half_rows, 1)
    sent = lax.dynamic_slice_in_dim(grid, (1 - branch) * half_rows, half_rows, 1)
    received = after(lax.ppermute(sent, "cfg", [(0, 1), (1, 0)]), text_out)
    conditional = jnp.where(branch == 0, kept, received)
    unconditional = jnp.where(branch == 0, received, kept)
    guided = unconditional + guidance[0] * (conditional - unconditional)
    return (guided, text_out[None])


def solution(mesh):
    devices = mesh.devices.reshape(mesh.devices.shape[:3] + (mesh.devices.shape[3] // 2, 2))
    split = Mesh(devices, ("cfg", "ta", "ha", "zh", "co"))
    wa = ("zh", "co")
    everyone = ("ta", "ha", "zh", "co")
    video = P("cfg", "ta", "ha", wa, None)
    in_specs = (
        video, video, video,
        P("cfg", None, None),
        P("cfg", everyone, None),
        P("cfg", everyone, None),
        P("cfg"),
        P(),
        video,
        P("cfg", None),
        P(),
        P("cfg", None, None),
        P(),
    )
    out_specs = (P("ta", ("ha", "cfg"), wa), P("cfg", None, None))
    return jax.shard_map(local, mesh=split, in_specs=in_specs, out_specs=out_specs, check_vma=False)
```

```python
import functools
import math

import jax
import jax.numpy as jnp
from jax import lax
from jax.experimental import pallas as pl
from jax.experimental.pallas import tpu as pltpu
from jax.sharding import Mesh
from jax.sharding import PartitionSpec as P

DEPTH = 128
WIDE = 3
NEVER = -(2.0**100)
CHIPS = ("ta", "ha", "zh")
SLOTS = 56
ENDS = 16
LOG2E = math.log2(math.e)
SCALE = LOG2E / math.sqrt(DEPTH)
MIB = 1024 * 1024

VMEM = pl.BlockSpec(memory_space=pltpu.VMEM)
SMEM = pl.BlockSpec(memory_space=pltpu.SMEM)
HBM = pl.BlockSpec(memory_space=pl.ANY)


def call(body, out_shape, in_specs, out_specs, scratch, vmem, flops, moved, *operands):
    return pl.pallas_call(
        body,
        grid=(1,),
        out_shape=out_shape,
        in_specs=in_specs,
        out_specs=out_specs,
        scratch_shapes=scratch,
        compiler_params=pltpu.CompilerParams(vmem_limit_bytes=64 * MIB - 65536),
        cost_estimate=pl.CostEstimate(flops=flops, bytes_accessed=moved, transcendentals=0),
    )(*operands)


def lanes(head):
    return pl.ds(pl.multiple_of(head * DEPTH, DEPTH), DEPTH)


def wide_heads(windows):
    found = jnp.int32(0)
    ids = [jnp.int32(0)] * WIDE
    for head in range(windows.shape[1]):
        wide = (windows[0, head] > 1) | (windows[1, head] > 1) | (windows[2, head] > 1)
        for at in range(WIDE):
            ids[at] = jnp.where(wide & (found == at), head, ids[at])
        found = found + wide.astype(jnp.int32)
    return ids


def outer(a, b):
    return lax.dot_general(a, b, (((1,), (1,)), ((), ())), preferred_element_type=jnp.float32)


def inner(a, b):
    return jnp.dot(a, b, preferred_element_type=jnp.float32)


def low(x):
    return x.astype(jnp.bfloat16)


def high(x):
    return x.astype(jnp.float32)


def slot(index):
    return pl.ds(index, 64, stride=SLOTS), slice(None)


def after_body(*refs):
    pass


def after(x, *others):
    return pl.pallas_call(
        after_body,
        out_shape=jax.ShapeDtypeStruct(x.shape, x.dtype),
        in_specs=[HBM] * (1 + len(others)),
        out_specs=HBM,
        input_output_aliases={0: 0},
    )(x, *others)


def front_body(
    windows, text, query, key_at, value_at, weight,
    pairs, queries, quarter, own_sums, far_sums, own_stats, far_stats,
    key, value, held, stats, passing, sems, weight_sems,
):
    ids = wide_heads(windows)
    tokens = query.shape[0]
    copies = [
        pltpu.make_async_copy(key_at, key, sems.at[WIDE]),
        pltpu.make_async_copy(value_at, value, sems.at[WIDE + 1]),
    ]
    for at in range(WIDE):
        copies.append(pltpu.make_async_copy(query.at[:, lanes(ids[at])], held.at[at], sems.at[at]))
    for copy in copies:
        copy.start()
    core = lax.axis_index("co")
    rows = quarter.shape[0]
    chunk = rows // 4
    loads = []
    stores = []
    for at in range(4):
        source = pl.ds(pl.multiple_of(core * rows + at * chunk, chunk), chunk)
        here = pl.ds(at * chunk, chunk)
        loads.append(
            pltpu.make_async_copy(weight.at[source, :], passing.at[here], weight_sems.at[0, at])
        )
        stores.append(
            pltpu.make_async_copy(passing.at[here], quarter.at[here], weight_sems.at[1, at])
        )
    for copy in copies:
        copy.wait()
    for load in loads:
        load.start()
    for at in range(WIDE):
        queries[at] = held[at].T
        pairs[at] = key[:, lanes(ids[at])]
        picked = value[:, lanes(ids[at])]
        for row in range(0, tokens, DEPTH):
            pairs[WIDE + at, row : row + DEPTH] = picked[row : row + DEPTH].T
    half = own_sums.shape[0]
    own_rows = pl.ds(pl.multiple_of(core * half, half), half)
    far_rows = pl.ds(pl.multiple_of((1 - core) * half, half), half)
    stats[...] = jnp.zeros(stats.shape, jnp.float32)
    for head in range(text.shape[1] // DEPTH):
        if head % 3 == 2:
            loads[head // 3].wait()
            stores[head // 3].start()
        cols = slice(head * DEPTH, (head + 1) * DEPTH)
        asked = jnp.concatenate((text[own_rows, cols], text[far_rows, cols]), axis=0).T
        scores = inner(key[:, cols], asked) * SCALE
        peak = jnp.max(scores, axis=0, keepdims=True)
        weights = jnp.exp2(scores - peak)
        stats[head : head + 1] = peak
        stats[16 + head : 17 + head] = jnp.sum(weights, axis=0, keepdims=True)
        mixed = inner(low(weights).T, value[:, cols])
        own_sums[:, cols] = mixed[:half]
        far_sums[:, cols] = mixed[half:]
    turned = stats[...].T
    own_stats[...] = turned[:half]
    far_stats[...] = turned[half:]
    for store in stores:
        store.wait()


def text_join_body(sums, stats, far_sums, far_stats, text_key, text_value, *rest):
    parcel, out = rest[-2:]
    half, width = sums.shape
    heads = width // DEPTH
    lane = lax.broadcasted_iota(jnp.int32, stats.shape, 1)
    held = jnp.zeros(stats.shape, jnp.float32)
    for head in range(heads):
        cols = slice(head * DEPTH, (head + 1) * DEPTH)
        first, second = stats[:, head : head + 1], far_stats[:, head : head + 1]
        top = high(low(jnp.maximum(first, second)))
        first, second = jnp.exp2(first - top), jnp.exp2(second - top)
        total = stats[:, 16 + head : 17 + head] * first + far_stats[:, 16 + head : 17 + head] * second
        mixed = sums[:, cols] * first + far_sums[:, cols] * second
        coarse = high(low(mixed))
        out[slot(head)] = coarse
        out[slot(heads + head)] = mixed - coarse
        big = high(low(total))
        held = jnp.where(lane == head, top, held)
        held = jnp.where(lane == 16 + head, big, held)
        held = jnp.where(lane == 32 + head, total - big, held)
        out[slot(2 * heads + 1 + head)] = jnp.broadcast_to(high(text_key[:, cols]), (half, DEPTH))
        out[slot(3 * heads + 1 + head)] = jnp.broadcast_to(high(text_value[:, cols]), (half, DEPTH))
    out[slot(2 * heads)] = held
    spare = jnp.zeros((half, DEPTH), jnp.float32)
    for index in range(4 * heads + 1, SLOTS):
        out[slot(index)] = spare
    parcel[...] = low(out[...])


def text_masks(count, rows, cols):
    place = 2 * lax.broadcasted_iota(jnp.int32, (rows, cols), 0)
    core = lax.axis_index("co")
    return place + core < count, place + 1 - core < count


def back_body(
    windows, count, text, query, key, value, queries, got_low, got_other_low, after,
    finished, out, sums, stats, text_keys, text_values, ids, got, got_other,
):
    got[...] = high(got_low[...])
    got_other[...] = high(got_other_low[...])
    text_merge(text, count, got, got_other, finished)
    heads = windows.shape[1]
    half = got.shape[0] // SLOTS
    for head in range(heads):
        for at, source in enumerate((got, got_other)):
            rows = slice(at * half, (at + 1) * half)
            text_keys[head, rows] = low(source[slot(2 * heads + 1 + head)])
            text_values[head, rows] = low(source[slot(3 * heads + 1 + head)])
    found = jnp.int32(0)
    for head in range(heads):
        wide = (windows[0, head] > 1) | (windows[1, head] > 1) | (windows[2, head] > 1)
        ids[jnp.where(wide, heads, found)] = head
        found = found + 1 - wide.astype(jnp.int32)
    tokens = query.shape[0]
    valid = jnp.concatenate(
        [high(mask.astype(jnp.int32)) for mask in text_masks(count[0], half, DEPTH)], axis=0
    ) > 0.5

    def step(group, carry):
        for at in range(3):
            head = ids[group * 3 + at]
            cols = lanes(head)
            keys = jnp.concatenate((key[:, cols], text_keys[head]), axis=0)
            values = jnp.concatenate((value[:, cols], text_values[head]), axis=0).T
            asked = query[:, cols].T
            for first in range(0, tokens, DEPTH):
                scores = inner(keys, asked[:, first : first + DEPTH]) * SCALE
                near, text = scores[:tokens], jnp.where(valid, scores[tokens:], NEVER)
                peak = jnp.maximum(
                    jnp.max(near, axis=0, keepdims=True), jnp.max(text, axis=0, keepdims=True)
                )
                weights = jnp.exp2(jnp.concatenate((near, text), axis=0) - peak)
                total = jnp.sum(weights, axis=0, keepdims=True)
                mixed = inner(values, low(weights))
                out[first : first + DEPTH, cols] = low((mixed / total).T)
        return carry

    lax.fori_loop(0, (heads - WIDE) // 3, step, 0)
    row = lax.broadcasted_iota(jnp.int32, (stats.shape[1], DEPTH), 0)
    for at, head in enumerate(wide_heads(windows)):
        keys = text_keys[head]
        values = text_values[head].T
        for first in range(0, tokens, DEPTH):
            some = slice(first, first + DEPTH)
            scores = jnp.where(valid, inner(keys, queries[at, :, some]) * SCALE, NEVER)
            peak = jnp.max(scores, axis=0, keepdims=True)
            weights = jnp.exp2(scores - peak)
            stats[at, :, some] = jnp.where(row == 0, peak, jnp.sum(weights, axis=0, keepdims=True))
            sums[at, :, some] = inner(values, low(weights))


def place_ok(windows, head, a, c):
    row_at, zone, core = lax.axis_index("ha"), lax.axis_index("zh"), lax.axis_index("co")
    ok = jnp.bool_(True)
    if a > 0:
        ok = windows[1, head] > 1
        ok = ok & ((row_at > 0) if a == 1 else (row_at < lax.axis_size("ha") - 1))
    if c > 0:
        ok = ok & (windows[2, head] > 1)
    if c == 1:
        ok = ok & jnp.where(core == 0, zone > 0, zone < lax.axis_size("zh") - 1)
    return ok


def wide_walk(
    windows, tables, asked, before, keys, values, peak, total, mixed, counts, sems, finish
):
    ids = wide_heads(windows)
    tokens = asked[0].shape[2]
    places = list(tables)
    for at in range(WIDE):
        found = jnp.int32(0)
        for number, (a, c) in enumerate(places):
            source = tables[a, c]
            ok = place_ok(windows, ids[at], a, c)
            slot_at = at * len(places) + number
            rows = pl.ds(pl.multiple_of(found * tokens, tokens), tokens)

            @pl.when(ok)
            def _(source=source, slot_at=slot_at, rows=rows, at=at):
                pltpu.make_async_copy(source.at[at], keys.at[at, rows], sems.at[slot_at, 0]).start()
                pltpu.make_async_copy(
                    source.at[WIDE + at], values.at[at, rows], sems.at[slot_at, 1]
                ).start()

            found = found + ok.astype(jnp.int32)
        counts[at] = found
        counts[WIDE + at] = ids[at]
    any_tile = tables[places[0]]

    def head_step(at, carry):
        head = counts[WIDE + at]
        count = counts[at]
        for number, (a, c) in enumerate(places):

            @pl.when(place_ok(windows, head, a, c))
            def _(number=number):
                slot_at = at * len(places) + number
                whole = pl.ds(0, tokens)
                pltpu.make_async_copy(any_tile.at[0], keys.at[at, whole], sems.at[slot_at, 0]).wait()
                pltpu.make_async_copy(any_tile.at[0], values.at[at, whole], sems.at[slot_at, 1]).wait()

        before(at)

        def span(start, size, sources):
            rows = pl.ds(pl.multiple_of(start, tokens), size)
            key = keys[at, rows]
            value = values[at, rows]
            value = jnp.concatenate(
                [value[row : row + DEPTH] for row in range(0, size, DEPTH)], axis=1
            )
            for part, source in sources:
                for first in range(0, tokens, DEPTH):
                    some = slice(part * tokens + first, part * tokens + first + DEPTH)
                    scores = inner(key, source[at, :, first : first + DEPTH]) * SCALE
                    held = peak[:, some]
                    top = jnp.maximum(held, jnp.max(scores, axis=0, keepdims=True))
                    factor = jnp.exp2(held - top)
                    weights = jnp.exp2(scores - top)
                    total[:, some] = total[:, some] * factor + jnp.sum(
                        weights, axis=0, keepdims=True
                    )
                    mixed[:, some] = mixed[:, some] * factor + inner(value, low(weights))
                    peak[:, some] = top

        def spans(sources):
            @pl.when(count == len(places))
            def _():
                span(0, len(places) * tokens, sources)

            @pl.when(count < len(places))
            def _():
                threes = count // 3 if len(places) > 3 else 0

                def three(step, carry):
                    span(step * 3 * tokens, 3 * tokens, sources)
                    return carry

                def one(step, carry):
                    span(step * tokens, tokens, sources)
                    return carry

                if len(places) > 3:
                    lax.fori_loop(0, threes, three, 0)
                lax.fori_loop(threes * 3, count, one, 0)

        spans(((0, asked[0]),))

        @pl.when(windows[0, head] > 1)
        def _():
            spans(((1, asked[1]), (2, asked[2])))

        finish(at)
        return carry

    lax.fori_loop(0, WIDE, head_step, 0)


def wide_near_body(
    windows, own, left, right, own_in, left_in, right_in, queries, before, after,
    sums, stats, keys, values, peak, total, mixed, counts, sems,
):
    def start(at):
        peak[...] = jnp.full(peak.shape, NEVER, jnp.float32)
        total[...] = jnp.zeros(total.shape, jnp.float32)
        mixed[...] = jnp.zeros(mixed.shape, jnp.float32)

    def finish(at):
        sums[at] = mixed[...]
        row = lax.broadcasted_iota(jnp.int32, stats.shape[1:], 0)
        stats[at] = jnp.where(row == 0, peak[...], total[...])

    tables = {
        (0, 0): own, (0, 2): own_in, (1, 0): left, (1, 2): left_in, (2, 0): right, (2, 2): right_in
    }
    asked = (queries, before, after)
    wide_walk(
        windows, tables, asked, start, keys, values, peak, total, mixed, counts, sems, finish
    )


def wide_far_body(
    windows, own, left, right, queries, before, after, held_sums, held_stats,
    sums, stats, out0, out1, keys, values, peak, total, mixed, counts, sems,
):
    tokens = queries.shape[2]

    def start(at):
        peak[...] = held_stats[at, 0:1]
        total[...] = held_stats[at, 1:2]
        mixed[...] = held_sums[at]

    def finish(at):
        sums[at] = mixed[:, :tokens]
        row = lax.broadcasted_iota(jnp.int32, stats.shape[1:], 0)
        stats[at] = jnp.where(row == 0, peak[:, :tokens], total[:, :tokens])
        for part, out in ((1, out0), (2, out1)):
            some = slice(part * tokens, (part + 1) * tokens)
            top = high(low(peak[:, some]))
            factor = jnp.exp2(peak[:, some] - top)
            whole = total[:, some] * factor
            big = high(low(whole))
            row = lax.broadcasted_iota(jnp.int32, (16, tokens), 0)
            held = jnp.where(row == 0, top, jnp.where(row == 1, big, whole - big))
            out[at, :DEPTH] = low(mixed[:, some] * factor)
            out[at, DEPTH:] = low(held)

    tables = {(0, 1): own, (1, 1): left, (2, 1): right}
    asked = (queries, before, after)
    wide_walk(
        windows, tables, asked, start, keys, values, peak, total, mixed, counts, sems, finish
    )


def text_merge(query, count, got, got_other, out):
    heads = query.shape[1] // DEPTH
    core = lax.axis_index("co")
    chip = (
        lax.axis_index("ta") * lax.axis_size("ha") + lax.axis_index("ha")
    ) * lax.axis_size("zh") + lax.axis_index("zh")
    sources = got.shape[0] // SLOTS
    at = core * sources + chip
    block = high(query[pl.ds(pl.multiple_of(at // 16 * 16, 16), 16), :])
    row = lax.broadcasted_iota(jnp.int32, block.shape, 0)
    asked = jnp.sum(jnp.where(row == at % 16, block, 0.0), axis=0, keepdims=True)
    near, far = text_masks(count[0], sources, 1)
    stats = got[slot(2 * heads)]
    blocks = []
    for head in range(heads):
        peak = stats[:, head : head + 1]
        mine = asked[:, head * DEPTH : (head + 1) * DEPTH]
        key_at, value_at = slot(2 * heads + 1 + head), slot(3 * heads + 1 + head)
        first = jnp.sum(got[key_at] * mine, axis=1, keepdims=True) * SCALE
        second = jnp.sum(got_other[key_at] * mine, axis=1, keepdims=True) * SCALE
        first = jnp.where(near, first, NEVER)
        second = jnp.where(far, second, NEVER)
        top = jnp.max(jnp.maximum(peak, jnp.maximum(first, second)), axis=0, keepdims=True)
        factor = jnp.exp2(peak - top)
        first = jnp.exp2(first - top)
        second = jnp.exp2(second - top)
        whole = jnp.sum(
            factor * (stats[:, 16 + head : 17 + head] + stats[:, 32 + head : 33 + head])
            + first
            + second,
            axis=0,
            keepdims=True,
        )
        mixed = jnp.sum(
            factor * (got[slot(head)] + got[slot(heads + head)]) + first * got[value_at] + second * got_other[value_at],
            axis=0,
            keepdims=True,
        )
        blocks.append(mixed / whole)
    blocks.append(jnp.zeros((ENDS - heads, DEPTH), jnp.float32))
    chunk = low(jnp.concatenate(blocks, axis=0))
    for source in range(sources):
        out[source * ENDS : (source + 1) * ENDS] = chunk


def text_out_body(mine, other, out, held):
    half = mine.shape[0] // ENDS
    held[0] = high(mine[...])
    held[1] = high(other[...])
    heads = out.shape[1] // DEPTH
    core = lax.axis_index("co")
    for source, place in ((0, core), (1, 1 - core)):
        rows = pl.ds(pl.multiple_of(place * half, half), half)
        for head in range(heads):
            picked = held[source, pl.ds(head, half, stride=ENDS), :]
            out[rows, head * DEPTH : (head + 1) * DEPTH] = low(picked)


def final_body(
    windows, sums, stats, text_sums, text_stats, back0, back1, narrow, w_own, w_mine, w_other,
    hidden, modulation, final, kept, sent, attended, weight, updated, residual,
    spread, sems, *, parts,
):
    ids = wide_heads(windows)
    branch, core = lax.axis_index("cfg"), lax.axis_index("co")
    half, model = w_own.shape
    part_cols = model // parts
    first = pltpu.make_async_copy(narrow, attended, sems.at[parts, 0])
    first.start()
    copies = []
    for part in range(parts):
        cols = pl.ds(part * part_cols, part_cols)
        for at, (source, row) in enumerate(
            (
                (w_own, branch * half),
                (w_mine, (1 - branch) * half + core * (half // 2)),
                (w_other, (1 - branch) * half + (1 - core) * (half // 2)),
            )
        ):
            rows = pl.ds(pl.multiple_of(row, half // 2), source.shape[0])
            copies.append(
                pltpu.make_async_copy(
                    source.at[:, cols], weight.at[rows, cols], sems.at[part, at]
                )
            )
        copies.append(
            pltpu.make_async_copy(hidden.at[:, cols], residual.at[:, cols], sems.at[part, 3])
        )
    for copy in copies:
        copy.start()
    time_at = lax.axis_index("ta")
    inside = (time_at > 0, time_at < lax.axis_size("ta") - 1)
    first.wait()
    for at in range(WIDE):
        peaks = [stats[at, 0:1], text_stats[at, 0:1]]
        totals = [stats[at, 1:2], text_stats[at, 1:2]]
        for back, ok in zip((back0, back1), inside):
            rows = high(back[at, DEPTH:])
            peaks.append(jnp.where(ok, rows[0:1], NEVER))
            totals.append(jnp.where(ok, rows[1:2] + rows[2:3], 0.0))
        top = functools.reduce(jnp.maximum, peaks)
        factors = [jnp.exp2(peak - top) for peak in peaks]
        total = sum(factor * whole for factor, whole in zip(factors, totals))
        mixed = (
            sums[at] * factors[0]
            + text_sums[at] * factors[1]
            + high(back0[at, :DEPTH]) * factors[2]
            + high(back1[at, :DEPTH]) * factors[3]
        )
        attended[:, lanes(ids[at])] = low((mixed / total).T)
    tokens = attended.shape[0]
    pivot = None
    running = jnp.zeros((tokens, DEPTH), jnp.float32)
    squares = jnp.zeros((tokens, DEPTH), jnp.float32)
    for part in range(parts):
        cols = slice(part * part_cols, (part + 1) * part_cols)
        for copy in copies[4 * part : 4 * part + 4]:
            copy.wait()
        projected = inner(attended[...], weight[:, cols])
        fresh = high(residual[:, cols]) + modulation[0, :, cols] * projected
        if pivot is None:
            pivot = jnp.sum(fresh, axis=1, keepdims=True) / part_cols
        fresh = fresh - pivot
        updated[:, cols] = fresh
        for lane in range(0, part_cols, DEPTH):
            some = fresh[:, lane : lane + DEPTH]
            running = running + some
            squares = squares + some * some
    mean = jnp.sum(running, axis=1, keepdims=True) / model
    variance = jnp.sum(squares, axis=1, keepdims=True) / model - mean * mean
    factor = lax.rsqrt(jnp.maximum(variance, 0.0) + 1e-06)
    channels = final.shape[0]
    result = jnp.zeros((tokens, channels), jnp.float32)
    for part in range(parts):
        cols = slice(part * part_cols, (part + 1) * part_cols)
        normed = (updated[:, cols] - mean) * factor * (1.0 + modulation[2, :, cols])
        normed = normed + modulation[1, :, cols]
        result = result + outer(low(normed), final[:, cols])
    spread[:, :channels] = result
    frames, half_rows = kept.shape[:2]
    columns = kept.shape[2] // channels
    for out, place in ((kept, branch), (sent, 1 - branch)):
        for frame in range(frames):
            for column in range(columns):
                first = ((frame * 2 + place) * half_rows) * columns + column
                out[frame, :, column * channels : (column + 1) * channels] = spread[
                    pl.ds(first, half_rows, stride=columns), :
                ][:, :channels]


def shift(x, axis, step):
    size = lax.axis_size(axis)
    return lax.ppermute(x, axis, [(i, i + step) for i in range(size) if 0 <= i + step < size])


def swap_core(x):
    return lax.ppermute(x, "co", [(0, 1), (1, 0)])


def local(
    video_query, video_key, video_value, text_query, text_key, text_value, text_count, head_windows,
    hidden_state, out_weight, final_weight, modulation, guidance,
):
    frames, rows, cols, width = video_query.shape[1:]
    tokens = frames * rows * cols
    heads = head_windows.shape[0]
    text_len = text_query.shape[1]
    half_text = text_len // 2
    model = out_weight.shape[1]
    half_width = out_weight.shape[0]
    bf16, f32 = jnp.bfloat16, jnp.float32
    shape = jax.ShapeDtypeStruct
    query = video_query.reshape(tokens, width)
    key = video_key.reshape(tokens, width)
    value = video_value.reshape(tokens, width)
    text_query = text_query[0]
    windows = head_windows.T
    core = lax.axis_index("co")
    branch = lax.axis_index("cfg")
    zones = lax.axis_size("zh")
    branches = lax.axis_size("cfg")

    part_shape = shape((half_text, width), f32)
    stat_shape = shape((half_text, DEPTH), f32)
    pairs, queries, quarter, text_sums, far_sums, text_stats, far_stats = call(
        front_body,
        (
            shape((2 * WIDE, tokens, DEPTH), bf16), shape((WIDE, DEPTH, tokens), bf16),
            shape((half_width // 2, model), bf16), part_shape, part_shape, stat_shape, stat_shape,
        ),
        [SMEM, VMEM] + [HBM] * 4,
        (VMEM, VMEM, HBM) + (VMEM,) * 4,
        [
            pltpu.VMEM((tokens, width), bf16),
            pltpu.VMEM((tokens, width), bf16),
            pltpu.VMEM((WIDE, tokens, DEPTH), bf16),
            pltpu.VMEM((DEPTH, DEPTH), f32),
            pltpu.VMEM((half_width // 2, model), bf16),
            pltpu.SemaphoreType.DMA((WIDE + 2,)),
            pltpu.SemaphoreType.DMA((2, 4)),
        ],
        24, 0, 0,
        windows, text_query, query, key, value, out_weight,
    )
    beside = [(2 * z + 1, 2 * z + 2) for z in range(zones - 1)]
    beside = beside + [(b, a) for a, b in beside]
    next_pairs = lax.ppermute(pairs, ("zh", "co"), beside)
    pairs_in = swap_core(pairs)
    left = shift(pairs, "ha", 1)
    right = shift(pairs, "ha", -1)

    parcel = call(
        text_join_body,
        shape((SLOTS * half_text, DEPTH), bf16),
        [VMEM] * 6 + [HBM] * 2, VMEM, [pltpu.VMEM((SLOTS * half_text, DEPTH), f32)],
        16, 0, 2 * MIB,
        text_sums, text_stats, swap_core(far_sums), swap_core(far_stats), text_key[0], text_value[0],
        left, right,
    )

    next_left = shift(next_pairs, "ha", 1)
    next_right = shift(next_pairs, "ha", -1)
    left_in = swap_core(left)
    right_in = swap_core(right)

    def at(branch_at, zone, core_at):
        return (branch_at * zones + zone) * 2 + core_at

    weight_pairs = []
    for z in range(zones):
        weight_pairs.append((at(0, z, 0), at(1, z, 0)))
        weight_pairs.append((at(0, (z + 1) % zones, 1), at(1, z, 1)))
    weight_pairs = weight_pairs + [(b, a) for a, b in weight_pairs]
    queries = after(queries, parcel)
    from_before = shift(queries, "ta", 1)
    from_after = shift(queries, "ta", -1)
    parcel = after(parcel, next_pairs)
    got = lax.all_to_all(parcel, CHIPS, 0, 0, tiled=True)
    wide_sums = shape((WIDE, DEPTH, tokens), f32)
    wide_stats = shape((WIDE, 8, tokens), f32)
    lent = shape((WIDE, DEPTH + 16, tokens), bf16)
    def wide_scratch(places):
        return [
            pltpu.VMEM((WIDE, places * tokens, DEPTH), bf16),
            pltpu.VMEM((WIDE, places * tokens, DEPTH), bf16),
            pltpu.VMEM((1, 3 * tokens), f32),
            pltpu.VMEM((1, 3 * tokens), f32),
            pltpu.VMEM((DEPTH, 3 * tokens), f32),
            pltpu.SMEM((2 * WIDE,), jnp.int32),
            pltpu.SemaphoreType.DMA((WIDE * places, 2)),
        ]

    near_sums, near_stats = call(
        wide_near_body,
        (shape((WIDE, DEPTH, 3 * tokens), f32), shape((WIDE, 8, 3 * tokens), f32)),
        [SMEM] + [HBM] * 6 + [VMEM] * 3, (VMEM,) * 2,
        wide_scratch(6),
        24, 0, 0,
        windows, pairs, left, right, pairs_in, left_in, right_in, queries, from_before, from_after,
    )
    sums, stats, to_before, to_after = call(
        wide_far_body,
        (wide_sums, wide_stats, lent, lent),
        [SMEM] + [HBM] * 3 + [VMEM] * 5, (VMEM,) * 4,
        wide_scratch(3),
        24, 10**12, 0,
        windows, next_pairs, next_left, next_right, queries, from_before, from_after,
        near_sums, near_stats,
    )
    w_mine = lax.ppermute(after(quarter, near_stats), ("cfg", "zh", "co"), weight_pairs)
    back_after = shift(to_before, "ta", -1)
    back_before = shift(to_after, "ta", 1)

    got = after(got, to_before)
    got_other = swap_core(got)
    finished, narrow, beside_sums, beside_stats = call(
        back_body,
        (
            shape((ENDS * half_text, DEPTH), bf16), shape((tokens, width), bf16), wide_sums,
            wide_stats,
        ),
        [SMEM, SMEM] + [VMEM] * 7 + [HBM], (VMEM,) * 4,
        [
            pltpu.VMEM((heads, text_len, DEPTH), bf16),
            pltpu.VMEM((heads, text_len, DEPTH), bf16),
            pltpu.SMEM((heads + 1,), jnp.int32),
            pltpu.VMEM((SLOTS * half_text, DEPTH), f32),
            pltpu.VMEM((SLOTS * half_text, DEPTH), f32),
        ],
        24, 4 * (heads - WIDE) * tokens * (tokens + text_len) * DEPTH, 5 * tokens * width * 2,
        windows, text_count, text_query, query, key, value, queries, got, got_other, to_before,
    )
    finished = after(finished, back_before, back_after)
    w_mine = after(w_mine, finished)
    w_other = swap_core(w_mine)
    text_mine = lax.all_to_all(finished, CHIPS, 0, 0, tiled=True)

    parts = 6
    half_rows = rows // branches
    half_out = shape((frames, half_rows, cols * final_weight.shape[1]), f32)
    kept, sent = call(
        functools.partial(final_body, parts=parts),
        (half_out, half_out),
        [SMEM] + [VMEM] * 6 + [HBM] * 5 + [VMEM] * 2, (VMEM, VMEM),
        [
            pltpu.VMEM((tokens, width), bf16),
            pltpu.VMEM((width, model), bf16),
            pltpu.VMEM((tokens, model), f32),
            pltpu.VMEM((tokens, model), bf16),
            pltpu.VMEM((tokens, DEPTH), f32),
            pltpu.SemaphoreType.DMA((parts + 1, 4)),
        ],
        40, 2 * tokens * width * model, 16 * MIB,
        windows, sums, stats, beside_sums, beside_stats, back_before, back_after, narrow,
        out_weight, w_mine, w_other,
        hidden_state.reshape(tokens, model), modulation.transpose(1, 0, 2), final_weight.T,
    )
    text_mine = after(text_mine, kept)
    text_out = call(
        text_out_body, shape((text_len, width), bf16), [VMEM, VMEM], VMEM,
        [pltpu.VMEM((2, ENDS * half_text, DEPTH), f32)], 8, 0, MIB,
        text_mine, swap_core(text_mine),
    )
    received = after(lax.ppermute(sent, "cfg", [(0, 1), (1, 0)]), text_out)
    conditional = jnp.where(branch == 0, kept, received)
    unconditional = jnp.where(branch == 0, received, kept)
    guided = unconditional + guidance[0] * (conditional - unconditional)
    return (guided, text_out[None])


def solution(mesh):
    devices = mesh.devices.reshape(mesh.devices.shape[:3] + (mesh.devices.shape[3] // 2, 2))
    split = Mesh(devices, ("cfg", "ta", "ha", "zh", "co"))
    wa = ("zh", "co")
    everyone = ("ta", "ha", "zh", "co")
    video = P("cfg", "ta", "ha", wa, None)
    in_specs = (
        video, video, video,
        P("cfg", None, None),
        P("cfg", everyone, None),
        P("cfg", everyone, None),
        P("cfg"),
        P(),
        video,
        P("cfg", None),
        P(),
        P("cfg", None, None),
        P(),
    )
    out_specs = (P("ta", ("ha", "cfg"), wa), P("cfg", None, None))
    return jax.shard_map(local, mesh=split, in_specs=in_specs, out_specs=out_specs, check_vma=False)
```

```python
import functools
import math

import jax
import jax.numpy as jnp
from jax import lax
from jax.experimental import pallas as pl
from jax.experimental.pallas import tpu as pltpu
from jax.sharding import Mesh
from jax.sharding import PartitionSpec as P

DEPTH = 128
WIDE = 3
NEVER = -(2.0**100)
CHIPS = ("ta", "ha", "zh")
SLOTS = 56
ENDS = 16
LOG2E = math.log2(math.e)
SCALE = LOG2E / math.sqrt(DEPTH)
MIB = 1024 * 1024

VMEM = pl.BlockSpec(memory_space=pltpu.VMEM)
SMEM = pl.BlockSpec(memory_space=pltpu.SMEM)
HBM = pl.BlockSpec(memory_space=pl.ANY)


def call(body, out_shape, in_specs, out_specs, scratch, vmem, flops, moved, *operands):
    return pl.pallas_call(
        body,
        grid=(1,),
        out_shape=out_shape,
        in_specs=in_specs,
        out_specs=out_specs,
        scratch_shapes=scratch,
        compiler_params=pltpu.CompilerParams(vmem_limit_bytes=64 * MIB - 65536),
        cost_estimate=pl.CostEstimate(flops=flops, bytes_accessed=moved, transcendentals=0),
    )(*operands)


def lanes(head):
    return pl.ds(pl.multiple_of(head * DEPTH, DEPTH), DEPTH)


def wide_heads(windows):
    found = jnp.int32(0)
    ids = [jnp.int32(0)] * WIDE
    for head in range(windows.shape[1]):
        wide = (windows[0, head] > 1) | (windows[1, head] > 1) | (windows[2, head] > 1)
        for at in range(WIDE):
            ids[at] = jnp.where(wide & (found == at), head, ids[at])
        found = found + wide.astype(jnp.int32)
    return ids


def outer(a, b):
    return lax.dot_general(a, b, (((1,), (1,)), ((), ())), preferred_element_type=jnp.float32)


def inner(a, b):
    return jnp.dot(a, b, preferred_element_type=jnp.float32)


def low(x):
    return x.astype(jnp.bfloat16)


def high(x):
    return x.astype(jnp.float32)


def slot(index):
    return pl.ds(index, 64, stride=SLOTS), slice(None)


def after_body(*refs):
    pass


def after(x, *others):
    return pl.pallas_call(
        after_body,
        out_shape=jax.ShapeDtypeStruct(x.shape, x.dtype),
        in_specs=[HBM] * (1 + len(others)),
        out_specs=HBM,
        input_output_aliases={0: 0},
    )(x, *others)


def front_body(
    windows, text, query, key_at, value_at, weight,
    pairs, queries, quarter, own_sums, far_sums, own_stats, far_stats,
    key, value, held, stats, passing, sems, weight_sems,
):
    ids = wide_heads(windows)
    tokens = query.shape[0]
    copies = [
        pltpu.make_async_copy(key_at, key, sems.at[WIDE]),
        pltpu.make_async_copy(value_at, value, sems.at[WIDE + 1]),
    ]
    for at in range(WIDE):
        copies.append(pltpu.make_async_copy(query.at[:, lanes(ids[at])], held.at[at], sems.at[at]))
    for copy in copies:
        copy.start()
    core = lax.axis_index("co")
    rows = quarter.shape[0]
    chunk = rows // 4
    loads = []
    stores = []
    for at in range(4):
        source = pl.ds(pl.multiple_of(core * rows + at * chunk, chunk), chunk)
        here = pl.ds(at * chunk, chunk)
        loads.append(
            pltpu.make_async_copy(weight.at[source, :], passing.at[here], weight_sems.at[0, at])
        )
        stores.append(
            pltpu.make_async_copy(passing.at[here], quarter.at[here], weight_sems.at[1, at])
        )
    for copy in copies:
        copy.wait()
    for load in loads:
        load.start()
    for at in range(WIDE):
        queries[at] = held[at].T
        pairs[at] = key[:, lanes(ids[at])]
        picked = value[:, lanes(ids[at])]
        for row in range(0, tokens, DEPTH):
            pairs[WIDE + at, row : row + DEPTH] = picked[row : row + DEPTH].T
    half = own_sums.shape[0]
    own_rows = pl.ds(pl.multiple_of(core * half, half), half)
    far_rows = pl.ds(pl.multiple_of((1 - core) * half, half), half)
    stats[...] = jnp.zeros(stats.shape, jnp.float32)
    for head in range(text.shape[1] // DEPTH):
        if head % 3 == 2:
            loads[head // 3].wait()
            stores[head // 3].start()
        cols = slice(head * DEPTH, (head + 1) * DEPTH)
        asked = jnp.concatenate((text[own_rows, cols], text[far_rows, cols]), axis=0).T
        scores = inner(key[:, cols], asked) * SCALE
        peak = jnp.max(scores, axis=0, keepdims=True)
        weights = jnp.exp2(scores - peak)
        stats[head : head + 1] = peak
        stats[16 + head : 17 + head] = jnp.sum(weights, axis=0, keepdims=True)
        mixed = inner(low(weights).T, value[:, cols])
        own_sums[:, cols] = mixed[:half]
        far_sums[:, cols] = mixed[half:]
    turned = stats[...].T
    own_stats[...] = turned[:half]
    far_stats[...] = turned[half:]
    for store in stores:
        store.wait()


def text_join_body(sums, stats, far_sums, far_stats, text_key, text_value, *rest):
    parcel, out = rest[-2:]
    half, width = sums.shape
    heads = width // DEPTH
    lane = lax.broadcasted_iota(jnp.int32, stats.shape, 1)
    held = jnp.zeros(stats.shape, jnp.float32)
    for head in range(heads):
        cols = slice(head * DEPTH, (head + 1) * DEPTH)
        first, second = stats[:, head : head + 1], far_stats[:, head : head + 1]
        top = high(low(jnp.maximum(first, second)))
        first, second = jnp.exp2(first - top), jnp.exp2(second - top)
        total = stats[:, 16 + head : 17 + head] * first + far_stats[:, 16 + head : 17 + head] * second
        mixed = sums[:, cols] * first + far_sums[:, cols] * second
        coarse = high(low(mixed))
        out[slot(head)] = coarse
        out[slot(heads + head)] = mixed - coarse
        big = high(low(total))
        held = jnp.where(lane == head, top, held)
        held = jnp.where(lane == 16 + head, big, held)
        held = jnp.where(lane == 32 + head, total - big, held)
        out[slot(2 * heads + 1 + head)] = jnp.broadcast_to(high(text_key[:, cols]), (half, DEPTH))
        out[slot(3 * heads + 1 + head)] = jnp.broadcast_to(high(text_value[:, cols]), (half, DEPTH))
    out[slot(2 * heads)] = held
    spare = jnp.zeros((half, DEPTH), jnp.float32)
    for index in range(4 * heads + 1, SLOTS):
        out[slot(index)] = spare
    parcel[...] = low(out[...])


def text_masks(count, rows, cols):
    place = 2 * lax.broadcasted_iota(jnp.int32, (rows, cols), 0)
    core = lax.axis_index("co")
    return place + core < count, place + 1 - core < count


def back_body(
    windows, count, text, query, key, value, queries, got_low, got_other_low, after,
    finished, out, sums, stats, text_keys, text_values, ids, got, got_other,
):
    got[...] = high(got_low[...])
    got_other[...] = high(got_other_low[...])
    text_merge(text, count, got, got_other, finished)
    heads = windows.shape[1]
    half = got.shape[0] // SLOTS
    for head in range(heads):
        for at, source in enumerate((got, got_other)):
            rows = slice(at * half, (at + 1) * half)
            text_keys[head, rows] = low(source[slot(2 * heads + 1 + head)])
            text_values[head, rows] = low(source[slot(3 * heads + 1 + head)])
    found = jnp.int32(0)
    for head in range(heads):
        wide = (windows[0, head] > 1) | (windows[1, head] > 1) | (windows[2, head] > 1)
        ids[jnp.where(wide, heads, found)] = head
        found = found + 1 - wide.astype(jnp.int32)
    tokens = query.shape[0]
    valid = jnp.concatenate(
        [high(mask.astype(jnp.int32)) for mask in text_masks(count[0], half, DEPTH)], axis=0
    ) > 0.5

    def step(group, carry):
        for at in range(3):
            head = ids[group * 3 + at]
            cols = lanes(head)
            keys = jnp.concatenate((key[:, cols], text_keys[head]), axis=0)
            values = jnp.concatenate((value[:, cols], text_values[head]), axis=0).T
            asked = query[:, cols].T
            for first in range(0, tokens, DEPTH):
                scores = inner(keys, asked[:, first : first + DEPTH]) * SCALE
                near, text = scores[:tokens], jnp.where(valid, scores[tokens:], NEVER)
                peak = jnp.maximum(
                    jnp.max(near, axis=0, keepdims=True), jnp.max(text, axis=0, keepdims=True)
                )
                weights = jnp.exp2(jnp.concatenate((near, text), axis=0) - peak)
                total = jnp.sum(weights, axis=0, keepdims=True)
                mixed = inner(values, low(weights))
                out[first : first + DEPTH, cols] = low((mixed / total).T)
        return carry

    lax.fori_loop(0, (heads - WIDE) // 3, step, 0)
    row = lax.broadcasted_iota(jnp.int32, (stats.shape[1], DEPTH), 0)
    for at, head in enumerate(wide_heads(windows)):
        keys = text_keys[head]
        values = text_values[head].T
        for first in range(0, tokens, DEPTH):
            some = slice(first, first + DEPTH)
            scores = jnp.where(valid, inner(keys, queries[at, :, some]) * SCALE, NEVER)
            peak = jnp.max(scores, axis=0, keepdims=True)
            weights = jnp.exp2(scores - peak)
            stats[at, :, some] = jnp.where(row == 0, peak, jnp.sum(weights, axis=0, keepdims=True))
            sums[at, :, some] = inner(values, low(weights))


def place_ok(windows, head, a, c):
    row_at, zone, core = lax.axis_index("ha"), lax.axis_index("zh"), lax.axis_index("co")
    ok = jnp.bool_(True)
    if a > 0:
        ok = windows[1, head] > 1
        ok = ok & ((row_at > 0) if a == 1 else (row_at < lax.axis_size("ha") - 1))
    if c > 0:
        ok = ok & (windows[2, head] > 1)
    if c == 1:
        ok = ok & jnp.where(core == 0, zone > 0, zone < lax.axis_size("zh") - 1)
    return ok


def wide_walk(
    windows, tables, asked, before, keys, values, peak, total, mixed, counts, sems, finish
):
    ids = wide_heads(windows)
    tokens = asked[0].shape[2]
    places = list(tables)
    for at in range(WIDE):
        found = jnp.int32(0)
        for number, (a, c) in enumerate(places):
            source = tables[a, c]
            ok = place_ok(windows, ids[at], a, c)
            slot_at = at * len(places) + number
            rows = pl.ds(pl.multiple_of(found * tokens, tokens), tokens)

            @pl.when(ok)
            def _(source=source, slot_at=slot_at, rows=rows, at=at):
                pltpu.make_async_copy(source.at[at], keys.at[at, rows], sems.at[slot_at, 0]).start()
                pltpu.make_async_copy(
                    source.at[WIDE + at], values.at[at, rows], sems.at[slot_at, 1]
                ).start()

            found = found + ok.astype(jnp.int32)
        counts[at] = found
        counts[WIDE + at] = ids[at]
    any_tile = tables[places[0]]

    def head_step(at, carry):
        head = counts[WIDE + at]
        count = counts[at]
        for number, (a, c) in enumerate(places):

            @pl.when(place_ok(windows, head, a, c))
            def _(number=number):
                slot_at = at * len(places) + number
                whole = pl.ds(0, tokens)
                pltpu.make_async_copy(any_tile.at[0], keys.at[at, whole], sems.at[slot_at, 0]).wait()
                pltpu.make_async_copy(any_tile.at[0], values.at[at, whole], sems.at[slot_at, 1]).wait()

        before(at)

        def span(start, size, sources):
            rows = pl.ds(pl.multiple_of(start, tokens), size)
            key = keys[at, rows]
            value = values[at, rows]
            value = jnp.concatenate(
                [value[row : row + DEPTH] for row in range(0, size, DEPTH)], axis=1
            )
            for part, source in sources:
                for first in range(0, tokens, DEPTH):
                    some = slice(part * tokens + first, part * tokens + first + DEPTH)
                    scores = inner(key, source[at, :, first : first + DEPTH]) * SCALE
                    held = peak[:, some]
                    top = jnp.maximum(held, jnp.max(scores, axis=0, keepdims=True))
                    factor = jnp.exp2(held - top)
                    weights = jnp.exp2(scores - top)
                    total[:, some] = total[:, some] * factor + jnp.sum(
                        weights, axis=0, keepdims=True
                    )
                    mixed[:, some] = mixed[:, some] * factor + inner(value, low(weights))
                    peak[:, some] = top

        def spans(sources):
            @pl.when(count == len(places))
            def _():
                span(0, len(places) * tokens, sources)

            @pl.when(count < len(places))
            def _():
                threes = count // 3 if len(places) > 3 else 0

                def three(step, carry):
                    span(step * 3 * tokens, 3 * tokens, sources)
                    return carry

                def one(step, carry):
                    span(step * tokens, tokens, sources)
                    return carry

                if len(places) > 3:
                    lax.fori_loop(0, threes, three, 0)
                lax.fori_loop(threes * 3, count, one, 0)

        spans(((0, asked[0]),))

        @pl.when(windows[0, head] > 1)
        def _():
            spans(((1, asked[1]), (2, asked[2])))

        finish(at)
        return carry

    lax.fori_loop(0, WIDE, head_step, 0)


def wide_near_body(
    windows, own, left, right, own_in, left_in, right_in, queries, before, after,
    sums, stats, keys, values, peak, total, mixed, counts, sems,
):
    def start(at):
        peak[...] = jnp.full(peak.shape, NEVER, jnp.float32)
        total[...] = jnp.zeros(total.shape, jnp.float32)
        mixed[...] = jnp.zeros(mixed.shape, jnp.float32)

    def finish(at):
        sums[at] = mixed[...]
        row = lax.broadcasted_iota(jnp.int32, stats.shape[1:], 0)
        stats[at] = jnp.where(row == 0, peak[...], total[...])

    tables = {
        (0, 0): own, (0, 2): own_in, (1, 0): left, (1, 2): left_in, (2, 0): right, (2, 2): right_in
    }
    asked = (queries, before, after)
    wide_walk(
        windows, tables, asked, start, keys, values, peak, total, mixed, counts, sems, finish
    )


def wide_far_body(
    windows, own, left, right, queries, before, after, held_sums, held_stats,
    sums, stats, out0, out1, keys, values, peak, total, mixed, counts, sems,
):
    tokens = queries.shape[2]

    def start(at):
        peak[...] = held_stats[at, 0:1]
        total[...] = held_stats[at, 1:2]
        mixed[...] = held_sums[at]

    def finish(at):
        sums[at] = mixed[:, :tokens]
        row = lax.broadcasted_iota(jnp.int32, stats.shape[1:], 0)
        stats[at] = jnp.where(row == 0, peak[:, :tokens], total[:, :tokens])
        for part, out in ((1, out0), (2, out1)):
            some = slice(part * tokens, (part + 1) * tokens)
            top = high(low(peak[:, some]))
            factor = jnp.exp2(peak[:, some] - top)
            whole = total[:, some] * factor
            big = high(low(whole))
            row = lax.broadcasted_iota(jnp.int32, (16, tokens), 0)
            held = jnp.where(row == 0, top, jnp.where(row == 1, big, whole - big))
            out[at, :DEPTH] = low(mixed[:, some] * factor)
            out[at, DEPTH:] = low(held)

    tables = {(0, 1): own, (1, 1): left, (2, 1): right}
    asked = (queries, before, after)
    wide_walk(
        windows, tables, asked, start, keys, values, peak, total, mixed, counts, sems, finish
    )


def text_merge(query, count, got, got_other, out):
    heads = query.shape[1] // DEPTH
    core = lax.axis_index("co")
    chip = (
        lax.axis_index("ta") * lax.axis_size("ha") + lax.axis_index("ha")
    ) * lax.axis_size("zh") + lax.axis_index("zh")
    sources = got.shape[0] // SLOTS
    at = core * sources + chip
    block = high(query[pl.ds(pl.multiple_of(at // 16 * 16, 16), 16), :])
    row = lax.broadcasted_iota(jnp.int32, block.shape, 0)
    asked = jnp.sum(jnp.where(row == at % 16, block, 0.0), axis=0, keepdims=True)
    near, far = text_masks(count[0], sources, 1)
    stats = got[slot(2 * heads)]
    blocks = []
    for head in range(heads):
        peak = stats[:, head : head + 1]
        mine = asked[:, head * DEPTH : (head + 1) * DEPTH]
        key_at, value_at = slot(2 * heads + 1 + head), slot(3 * heads + 1 + head)
        first = jnp.sum(got[key_at] * mine, axis=1, keepdims=True) * SCALE
        second = jnp.sum(got_other[key_at] * mine, axis=1, keepdims=True) * SCALE
        first = jnp.where(near, first, NEVER)
        second = jnp.where(far, second, NEVER)
        top = jnp.max(jnp.maximum(peak, jnp.maximum(first, second)), axis=0, keepdims=True)
        factor = jnp.exp2(peak - top)
        first = jnp.exp2(first - top)
        second = jnp.exp2(second - top)
        whole = jnp.sum(
            factor * (stats[:, 16 + head : 17 + head] + stats[:, 32 + head : 33 + head])
            + first
            + second,
            axis=0,
            keepdims=True,
        )
        mixed = jnp.sum(
            factor * (got[slot(head)] + got[slot(heads + head)]) + first * got[value_at] + second * got_other[value_at],
            axis=0,
            keepdims=True,
        )
        blocks.append(mixed / whole)
    blocks.append(jnp.zeros((ENDS - heads, DEPTH), jnp.float32))
    chunk = low(jnp.concatenate(blocks, axis=0))
    for source in range(sources):
        out[source * ENDS : (source + 1) * ENDS] = chunk


def text_out_body(mine, other, out, held):
    half = mine.shape[0] // ENDS
    held[0] = high(mine[...])
    held[1] = high(other[...])
    heads = out.shape[1] // DEPTH
    core = lax.axis_index("co")
    for source, place in ((0, core), (1, 1 - core)):
        rows = pl.ds(pl.multiple_of(place * half, half), half)
        for head in range(heads):
            picked = held[source, pl.ds(head, half, stride=ENDS), :]
            out[rows, head * DEPTH : (head + 1) * DEPTH] = low(picked)


def final_body(
    windows, sums, stats, text_sums, text_stats, back0, back1, narrow, w_own, w_mine, w_other,
    hidden, modulation, final, kept, sent, attended, weight, updated, residual,
    spread, sems, *, parts,
):
    ids = wide_heads(windows)
    branch, core = lax.axis_index("cfg"), lax.axis_index("co")
    half, model = w_own.shape
    part_cols = model // parts
    first = pltpu.make_async_copy(narrow, attended, sems.at[parts, 0])
    first.start()
    copies = []
    for part in range(parts):
        cols = pl.ds(part * part_cols, part_cols)
        for at, (source, row) in enumerate(
            (
                (w_own, branch * half),
                (w_mine, (1 - branch) * half + core * (half // 2)),
                (w_other, (1 - branch) * half + (1 - core) * (half // 2)),
            )
        ):
            rows = pl.ds(pl.multiple_of(row, half // 2), source.shape[0])
            copies.append(
                pltpu.make_async_copy(
                    source.at[:, cols], weight.at[rows, cols], sems.at[part, at]
                )
            )
        copies.append(
            pltpu.make_async_copy(hidden.at[:, cols], residual.at[:, cols], sems.at[part, 3])
        )
    for copy in copies:
        copy.start()
    time_at = lax.axis_index("ta")
    inside = (time_at > 0, time_at < lax.axis_size("ta") - 1)
    first.wait()
    for at in range(WIDE):
        peaks = [stats[at, 0:1], text_stats[at, 0:1]]
        totals = [stats[at, 1:2], text_stats[at, 1:2]]
        for back, ok in zip((back0, back1), inside):
            rows = high(back[at, DEPTH:])
            peaks.append(jnp.where(ok, rows[0:1], NEVER))
            totals.append(jnp.where(ok, rows[1:2] + rows[2:3], 0.0))
        top = functools.reduce(jnp.maximum, peaks)
        factors = [jnp.exp2(peak - top) for peak in peaks]
        total = sum(factor * whole for factor, whole in zip(factors, totals))
        mixed = (
            sums[at] * factors[0]
            + text_sums[at] * factors[1]
            + high(back0[at, :DEPTH]) * factors[2]
            + high(back1[at, :DEPTH]) * factors[3]
        )
        attended[:, lanes(ids[at])] = low((mixed / total).T)
    tokens = attended.shape[0]
    pivot = None
    running = jnp.zeros((tokens, DEPTH), jnp.float32)
    squares = jnp.zeros((tokens, DEPTH), jnp.float32)
    for part in range(parts):
        cols = slice(part * part_cols, (part + 1) * part_cols)
        for copy in copies[4 * part : 4 * part + 4]:
            copy.wait()
        projected = inner(attended[...], weight[:, cols])
        fresh = high(residual[:, cols]) + modulation[0, :, cols] * projected
        if pivot is None:
            pivot = jnp.sum(fresh, axis=1, keepdims=True) / part_cols
        fresh = fresh - pivot
        updated[:, cols] = fresh
        for lane in range(0, part_cols, DEPTH):
            some = fresh[:, lane : lane + DEPTH]
            running = running + some
            squares = squares + some * some
    mean = jnp.sum(running, axis=1, keepdims=True) / model
    variance = jnp.sum(squares, axis=1, keepdims=True) / model - mean * mean
    factor = lax.rsqrt(jnp.maximum(variance, 0.0) + 1e-06)
    channels = final.shape[0]
    result = jnp.zeros((tokens, channels), jnp.float32)
    for part in range(parts):
        cols = slice(part * part_cols, (part + 1) * part_cols)
        normed = (updated[:, cols] - mean) * factor * (1.0 + modulation[2, :, cols])
        normed = normed + modulation[1, :, cols]
        result = result + outer(low(normed), final[:, cols])
    spread[:, :channels] = result
    frames, half_rows = kept.shape[:2]
    columns = kept.shape[2] // channels
    for out, place in ((kept, branch), (sent, 1 - branch)):
        for frame in range(frames):
            for column in range(columns):
                first = ((frame * 2 + place) * half_rows) * columns + column
                out[frame, :, column * channels : (column + 1) * channels] = spread[
                    pl.ds(first, half_rows, stride=columns), :
                ][:, :channels]


def shift(x, axis, step):
    size = lax.axis_size(axis)
    return lax.ppermute(x, axis, [(i, i + step) for i in range(size) if 0 <= i + step < size])


def swap_core(x):
    return lax.ppermute(x, "co", [(0, 1), (1, 0)])


def local(
    video_query, video_key, video_value, text_query, text_key, text_value, text_count, head_windows,
    hidden_state, out_weight, final_weight, modulation, guidance,
):
    frames, rows, cols, width = video_query.shape[1:]
    tokens = frames * rows * cols
    heads = head_windows.shape[0]
    text_len = text_query.shape[1]
    half_text = text_len // 2
    model = out_weight.shape[1]
    half_width = out_weight.shape[0]
    bf16, f32 = jnp.bfloat16, jnp.float32
    shape = jax.ShapeDtypeStruct
    query = video_query.reshape(tokens, width)
    key = video_key.reshape(tokens, width)
    value = video_value.reshape(tokens, width)
    text_query = text_query[0]
    windows = head_windows.T
    core = lax.axis_index("co")
    branch = lax.axis_index("cfg")
    zones = lax.axis_size("zh")
    branches = lax.axis_size("cfg")

    part_shape = shape((half_text, width), f32)
    stat_shape = shape((half_text, DEPTH), f32)
    pairs, queries, quarter, text_sums, far_sums, text_stats, far_stats = call(
        front_body,
        (
            shape((2 * WIDE, tokens, DEPTH), bf16), shape((WIDE, DEPTH, tokens), bf16),
            shape((half_width // 2, model), bf16), part_shape, part_shape, stat_shape, stat_shape,
        ),
        [SMEM, VMEM] + [HBM] * 4,
        (VMEM, VMEM, HBM) + (VMEM,) * 4,
        [
            pltpu.VMEM((tokens, width), bf16),
            pltpu.VMEM((tokens, width), bf16),
            pltpu.VMEM((WIDE, tokens, DEPTH), bf16),
            pltpu.VMEM((DEPTH, DEPTH), f32),
            pltpu.VMEM((half_width // 2, model), bf16),
            pltpu.SemaphoreType.DMA((WIDE + 2,)),
            pltpu.SemaphoreType.DMA((2, 4)),
        ],
        24, 0, 0,
        windows, text_query, query, key, value, out_weight,
    )
    beside = [(2 * z + 1, 2 * z + 2) for z in range(zones - 1)]
    beside = beside + [(b, a) for a, b in beside]
    next_pairs = lax.ppermute(pairs, ("zh", "co"), beside)
    pairs_in = swap_core(pairs)
    left = shift(pairs, "ha", 1)
    right = shift(pairs, "ha", -1)

    parcel = call(
        text_join_body,
        shape((SLOTS * half_text, DEPTH), bf16),
        [VMEM] * 6 + [HBM] * 2, VMEM, [pltpu.VMEM((SLOTS * half_text, DEPTH), f32)],
        16, 0, 2 * MIB,
        text_sums, text_stats, swap_core(far_sums), swap_core(far_stats), text_key[0], text_value[0],
        left, right,
    )

    next_left = shift(next_pairs, "ha", 1)
    next_right = shift(next_pairs, "ha", -1)
    left_in = swap_core(left)
    right_in = swap_core(right)

    def at(branch_at, zone, core_at):
        return (branch_at * zones + zone) * 2 + core_at

    weight_pairs = []
    for z in range(zones):
        weight_pairs.append((at(0, z, 0), at(1, z, 0)))
        weight_pairs.append((at(0, (z + 1) % zones, 1), at(1, z, 1)))
    weight_pairs = weight_pairs + [(b, a) for a, b in weight_pairs]
    queries = after(queries, parcel)
    from_before = shift(queries, "ta", 1)
    from_after = shift(queries, "ta", -1)
    parcel = after(parcel, next_pairs)
    got = lax.all_to_all(parcel, CHIPS, 0, 0, tiled=True)
    wide_sums = shape((WIDE, DEPTH, tokens), f32)
    wide_stats = shape((WIDE, 8, tokens), f32)
    lent = shape((WIDE, DEPTH + 16, tokens), bf16)
    def wide_scratch(places):
        return [
            pltpu.VMEM((WIDE, places * tokens, DEPTH), bf16),
            pltpu.VMEM((WIDE, places * tokens, DEPTH), bf16),
            pltpu.VMEM((1, 3 * tokens), f32),
            pltpu.VMEM((1, 3 * tokens), f32),
            pltpu.VMEM((DEPTH, 3 * tokens), f32),
            pltpu.SMEM((2 * WIDE,), jnp.int32),
            pltpu.SemaphoreType.DMA((WIDE * places, 2)),
        ]

    near_sums, near_stats = call(
        wide_near_body,
        (shape((WIDE, DEPTH, 3 * tokens), f32), shape((WIDE, 8, 3 * tokens), f32)),
        [SMEM] + [HBM] * 6 + [VMEM] * 3, (VMEM,) * 2,
        wide_scratch(6),
        24, 0, 0,
        windows, pairs, left, right, pairs_in, left_in, right_in, queries, from_before, from_after,
    )
    sums, stats, to_before, to_after = call(
        wide_far_body,
        (wide_sums, wide_stats, lent, lent),
        [SMEM] + [HBM] * 3 + [VMEM] * 5, (VMEM,) * 4,
        wide_scratch(3),
        24, 10**12, 0,
        windows, next_pairs, next_left, next_right, queries, from_before, from_after,
        near_sums, near_stats,
    )
    w_mine = lax.ppermute(after(quarter, near_stats), ("cfg", "zh", "co"), weight_pairs)
    back_after = shift(to_before, "ta", -1)
    back_before = shift(to_after, "ta", 1)

    got = after(got, to_before)
    got_other = swap_core(got)
    finished, narrow, beside_sums, beside_stats = call(
        back_body,
        (
            shape((ENDS * half_text, DEPTH), bf16), shape((tokens, width), bf16), wide_sums,
            wide_stats,
        ),
        [SMEM, SMEM] + [VMEM] * 7 + [HBM], (VMEM,) * 4,
        [
            pltpu.VMEM((heads, text_len, DEPTH), bf16),
            pltpu.VMEM((heads, text_len, DEPTH), bf16),
            pltpu.SMEM((heads + 1,), jnp.int32),
            pltpu.VMEM((SLOTS * half_text, DEPTH), f32),
            pltpu.VMEM((SLOTS * half_text, DEPTH), f32),
        ],
        24, 4 * (heads - WIDE) * tokens * (tokens + text_len) * DEPTH, 5 * tokens * width * 2,
        windows, text_count, text_query, query, key, value, queries, got, got_other, to_before,
    )
    finished = after(finished, back_before, back_after)
    w_mine = after(w_mine, finished)
    w_other = swap_core(w_mine)
    text_mine = lax.all_to_all(finished, CHIPS, 0, 0, tiled=True)

    parts = 12
    half_rows = rows // branches
    half_out = shape((frames, half_rows, cols * final_weight.shape[1]), f32)
    kept, sent = call(
        functools.partial(final_body, parts=parts),
        (half_out, half_out),
        [SMEM] + [VMEM] * 6 + [HBM] * 5 + [VMEM] * 2, (VMEM, VMEM),
        [
            pltpu.VMEM((tokens, width), bf16),
            pltpu.VMEM((width, model), bf16),
            pltpu.VMEM((tokens, model), f32),
            pltpu.VMEM((tokens, model), bf16),
            pltpu.VMEM((tokens, DEPTH), f32),
            pltpu.SemaphoreType.DMA((parts + 1, 4)),
        ],
        40, 2 * tokens * width * model, 16 * MIB,
        windows, sums, stats, beside_sums, beside_stats, back_before, back_after, narrow,
        out_weight, w_mine, w_other,
        hidden_state.reshape(tokens, model), modulation.transpose(1, 0, 2), final_weight.T,
    )
    text_mine = after(text_mine, kept)
    text_out = call(
        text_out_body, shape((text_len, width), bf16), [VMEM, VMEM], VMEM,
        [pltpu.VMEM((2, ENDS * half_text, DEPTH), f32)], 8, 0, MIB,
        text_mine, swap_core(text_mine),
    )
    received = after(lax.ppermute(sent, "cfg", [(0, 1), (1, 0)]), text_out)
    conditional = jnp.where(branch == 0, kept, received)
    unconditional = jnp.where(branch == 0, received, kept)
    guided = unconditional + guidance[0] * (conditional - unconditional)
    return (guided, text_out[None])


def solution(mesh):
    devices = mesh.devices.reshape(mesh.devices.shape[:3] + (mesh.devices.shape[3] // 2, 2))
    split = Mesh(devices, ("cfg", "ta", "ha", "zh", "co"))
    wa = ("zh", "co")
    everyone = ("ta", "ha", "zh", "co")
    video = P("cfg", "ta", "ha", wa, None)
    in_specs = (
        video, video, video,
        P("cfg", None, None),
        P("cfg", everyone, None),
        P("cfg", everyone, None),
        P("cfg"),
        P(),
        video,
        P("cfg", None),
        P(),
        P("cfg", None, None),
        P(),
    )
    out_specs = (P("ta", ("ha", "cfg"), wa), P("cfg", None, None))
    return jax.shard_map(local, mesh=split, in_specs=in_specs, out_specs=out_specs, check_vma=False)
```
